128 devices in a mesh: shape: 8 (over z, core), grp: 16 (over y, x).
Axes of the slice: x: 4, y: 4, z: 4, core: 2. Of those that a mesh axis runs over, the one named last changes fastest.
Arguments:
- latents: bfloat16 [512, 64, 64, 128], P(('shape', 'grp')), parts along dimension 0, may hold values from -6 to 6
- up_weight: bfloat16 [3, 3, 3, 128, 64], replicated, may hold values from -0.25 to 0.25
- first_weight: bfloat16 [3, 3, 3, 64, 64], replicated, may hold values from -0.15625 to 0.15625
- second_weight: bfloat16 [3, 3, 3, 64, 64], replicated, may hold values from -0.15625 to 0.15625
- brick_ids: int32 [2048], P(('shape', 'grp')), parts along dimension 0, may hold values from -1 to 255, as said below
- brick_owner: int32 [2048], P(('shape', 'grp')), parts along dimension 0, may hold values from -1 to 15, as said below
- neighbor_live: int32 [2048, 27], P(('shape', 'grp')), parts along dimension 0, may hold values 0 or 1
Outputs:
- fine_bricks: bfloat16 [4096, 32768], P(('shape', 'grp')), parts along dimension 0
The draws below stay inside these ranges and needn't reach their ends.
There are 8 independent parts, one for each index of `shape`. The reference program is written for one: setup_inputs(seed, part) draws one part's arguments, and reference() takes and returns one part's arrays. A program takes and returns all parts, laid end to end along the dimension named above; an argument that names none is the same for every part. Nothing has to cross between parts.
Inputs may be any that keep to these rules, and one draw needn't show every extreme that they name: `brick_ids`: each device's block of 16 entries lists distinct bricks of its own panel by local number (x slowest, z fastest), -1 for an unused entry; every block uses 16 - 16 // 2 to 16 entries at any positions, and some block uses all of them. `brick_owner`: -1 exactly where brick_ids is -1. Within one device's block no owner appears more than 2 times among used entries, and one owner appears exactly 2 times among the used entries of every block.
All inputs are finite; a program needn't handle non-finite values. No bound on the sum of `neighbor_live` on one device may be relied on, other than what follows from the above.
Results may differ from the reference program's by a relative error of at most 0.0052.
Values may be sent and summed in bfloat16 or wider, within the bound.
A program may use at most 128 MiB of HBM per device.

```python
import jax
import jax.numpy as jnp
from jax import lax

C1 = 128
C2 = 64
BE = 8
HB = 4
G = 64
PX = 4
BPD = 16
SCAP = 2
OWN_ROWS = 32
OUT_ROWS = 512
GX = 64
BRICKS = 256
N_GRP = 16


def brick_lists(key):
    base_key = jax.random.fold_in(key, 4242)
    split_keys = jax.random.split(base_key, 6)
    panel_count = PX // HB * (G // HB) * (G // HB)
    used_counts = BPD - jax.random.randint(split_keys[0], (N_GRP,), 0, BPD // 2 + 1)
    full_device = jax.random.randint(split_keys[1], (), 0, N_GRP)
    used_counts = jnp.where(jnp.arange(N_GRP) == full_device, BPD, used_counts)
    hot_owner = jax.random.randint(split_keys[2], (), 0, N_GRP).astype(jnp.int32)
    other_owners = (jnp.arange((N_GRP - 1) * SCAP) // SCAP).astype(jnp.int32)
    other_owners = other_owners + (other_owners >= hot_owner).astype(jnp.int32)

    def per_device(cell_key, pool_key, order_key, used_count):
        brick_cells = jax.random.permutation(cell_key, panel_count)[:BPD]
        brick_cells = (brick_cells + (panel_count - 1 - brick_cells[0])) % panel_count
        chosen = jax.random.permutation(pool_key, other_owners)[:BPD - SCAP]
        owner_list = jnp.concatenate([jnp.full((SCAP,), hot_owner, jnp.int32), chosen.astype(jnp.int32)])
        slot_order = jax.random.permutation(order_key, BPD)
        used_slot = slot_order < used_count
        brick_list = jnp.where(used_slot, brick_cells[slot_order], -1)
        owner_slots = jnp.where(used_slot, owner_list[slot_order], -1)
        return (brick_list.astype(jnp.int32), owner_slots.astype(jnp.int32))
    brick_list, owner_slots = jax.vmap(per_device)(jax.random.split(split_keys[3], N_GRP), jax.random.split(split_keys[4], N_GRP), jax.random.split(split_keys[5], N_GRP), used_counts)
    return (brick_list.reshape(-1), owner_slots.reshape(-1))


def draw_brick_ids(key, part):
    return brick_lists(key)[0]


def draw_brick_owner(key, part):
    return brick_lists(key)[1]


def set_ends(values, key, least, top_value):
    longest = values.shape.index(max(values.shape))
    spots = []
    for shift in (0, 1):
        where = [jax.random.randint(jax.random.fold_in(key, axis), (), 0, length) for axis, length in enumerate(values.shape)]
        where[longest] = (where[longest] + shift) % values.shape[longest]
        spots.append(tuple(where))
    return values.at[spots[0]].set(least).at[spots[1]].set(top_value)


def levels(own_key, dims, shards, low, top_value):
    def one(position, parts):
        steps = jax.random.uniform(jax.random.fold_in(jax.random.fold_in(own_key, 6), position), (parts,), jnp.float32, low / len(shards), top_value / len(shards))
        return jnp.repeat(jnp.exp(steps), dims[position] // parts).reshape((-1,) + (1,) * (len(dims) - position - 1))

    level = one(*shards[0])
    for cut in shards[1:]:
        level = level * one(*cut)
    return level


def noise(key, dims, width, limit, cuts=(), kind=jnp.bfloat16):
    values = width * jax.random.normal(key, dims, jnp.float32)
    if cuts:
        values = values * levels(key, dims, cuts, -0.22, 0.18)
    return jnp.clip(values, -limit, limit).astype(kind)


def setup_inputs(seed: int = 0, part: int = 0) -> dict:
    streams_of = jax.random.split(jax.random.key(seed), 8)
    own_keys = jax.random.split(jax.random.fold_in(streams_of[7], part), 8)
    latents = noise(own_keys[0], (GX, G, G, C1), 1.0, 6.0, ((0, 16),))
    up_weight = noise(streams_of[1], (3, 3, 3, C1, C2), (4 * C1) ** -0.5, 0.25)
    first_weight = noise(streams_of[2], (3, 3, 3, C2, C2), (27 * C2) ** -0.5, 0.15625)
    second_weight = noise(streams_of[3], (3, 3, 3, C2, C2), (27 * C2) ** -0.5, 0.15625)
    brick_ids = draw_brick_ids(jax.random.fold_in(jax.random.fold_in(streams_of[7], part), 71), part)
    brick_owner = draw_brick_owner(jax.random.fold_in(jax.random.fold_in(streams_of[7], part), 71), part)
    neighbor_live = set_ends((jax.random.randint(own_keys[6], (BRICKS, 27), 0, 3) < 2).astype(jnp.int32), jax.random.fold_in(own_keys[6], 1), 0, 1)
    return dict(latents=latents, up_weight=up_weight, first_weight=first_weight, second_weight=second_weight, brick_ids=brick_ids, brick_owner=brick_owner, neighbor_live=neighbor_live)


parity_taps = (((1, 0),), ((2, 0), (0, 1)))


def upsample(regions, weight):
    sub_edge = regions.shape[1] - 1
    parity_grids = []
    for parity_x in range(2):
        plane_list = []
        for parity_y in range(2):
            line_list = []
            for parity_z in range(2):
                pieces = []
                kernels = []
                for tap_x, shift_x in parity_taps[parity_x]:
                    for tap_y, shift_y in parity_taps[parity_y]:
                        for tap_z, shift_z in parity_taps[parity_z]:
                            pieces.append(regions[:, shift_x:shift_x + sub_edge, shift_y:shift_y + sub_edge, shift_z:shift_z + sub_edge, :])
                            kernels.append(weight[tap_x, tap_y, tap_z])
                stacked = jnp.concatenate(pieces, axis=-1).astype(jnp.float32)
                kernel = jnp.concatenate(kernels, axis=0).astype(jnp.float32)
                line_list.append(jnp.einsum("bxyzc,co->bxyzo", stacked, kernel, precision=lax.Precision.HIGHEST))
            plane_list.append(jnp.stack(line_list, axis=4))
        parity_grids.append(jnp.stack(plane_list, axis=3))
    alternated = jnp.stack(parity_grids, axis=2)
    return alternated.reshape(regions.shape[0], 2 * sub_edge, 2 * sub_edge, 2 * sub_edge, weight.shape[-1])


def cell_mask(live_flags, full_edge):
    cell_pos = jnp.arange(full_edge, dtype=jnp.int32)
    neighbor_class = (cell_pos >= 2).astype(jnp.int32) + (cell_pos >= full_edge - 2).astype(jnp.int32)
    selector = (neighbor_class[:, None] == jnp.arange(3, dtype=jnp.int32)[None, :]).astype(jnp.float32)
    flag_cube = live_flags.reshape(live_flags.shape[0], 3, 3, 3)
    return jnp.einsum("bijk,xi,yj,zk->bxyz", flag_cube, selector, selector, selector, precision=lax.Precision.HIGHEST)


def conv_valid(inputs, kernel):
    return lax.conv_general_dilated(inputs.astype(jnp.float32), kernel.astype(jnp.float32), (1, 1, 1), "VALID", dimension_numbers=("NDHWC", "DHWIO", "NDHWC"), precision=lax.Precision.HIGHEST)


def refine(extended, full_mask, first_weight, second_weight):
    first_out = conv_valid(extended, first_weight)
    hidden = (jax.nn.silu(first_out) * full_mask[:, 1:-1, 1:-1, 1:-1, None]).astype(jnp.bfloat16)
    second_out = conv_valid(hidden, second_weight)
    refined = extended[:, 2:-2, 2:-2, 2:-2, :].astype(jnp.float32) + second_out
    return refined.astype(jnp.bfloat16).reshape(extended.shape[0], -1)


def neighbor_flags(brick_x, brick_y, brick_z, in_use, neighbor_live, bricks_long, bricks_across):
    offsets = jnp.arange(27, dtype=jnp.int32)
    step_x = offsets // 9 - 1
    step_y = (offsets // 3) % 3 - 1
    step_z = offsets % 3 - 1
    near_x = brick_x[:, None] + step_x[None, :]
    near_y = brick_y[:, None] + step_y[None, :]
    near_z = brick_z[:, None] + step_z[None, :]
    inside = (near_x >= 0) & (near_x < bricks_long) & (near_y >= 0) & (near_y < bricks_across) & (near_z >= 0) & (near_z < bricks_across)
    chosen = (neighbor_live > 0) | (offsets == 13)[None, :]
    return (inside & chosen & in_use[:, None]).astype(jnp.float32)


def reference(latents, up_weight, first_weight, second_weight, brick_ids, brick_owner, neighbor_live):
    across = G // HB
    panel_bricks = PX // HB
    padded = jnp.pad(latents, ((1, 2), (1, 2), (1, 2), (0, 0)))
    ids_block = brick_ids.reshape(N_GRP, BPD)
    owner_block = brick_owner.reshape(N_GRP, BPD)
    live_block = neighbor_live.reshape(N_GRP, BPD, 27)

    def one_device(inputs):
        device_pos, device_ids, device_live = inputs
        in_use = device_ids >= 0
        safe_ids = jnp.maximum(device_ids, 0).astype(jnp.int32)
        brick_x = (device_pos * panel_bricks + safe_ids // (across * across)).astype(jnp.int32)
        brick_y = ((safe_ids // across) % across).astype(jnp.int32)
        brick_z = (safe_ids % across).astype(jnp.int32)

        def slice_region(start_x, start_y, start_z):
            starts = ((start_x * HB).astype(jnp.int32), (start_y * HB).astype(jnp.int32), (start_z * HB).astype(jnp.int32), jnp.int32(0))
            return lax.dynamic_slice(padded, starts, (HB + 3, HB + 3, HB + 3, C1))

        regions = jax.vmap(slice_region)(brick_x, brick_y, brick_z)
        live_flags = neighbor_flags(brick_x, brick_y, brick_z, in_use, device_live, panel_bricks * N_GRP, across)
        full_mask = cell_mask(live_flags, BE + 4)
        extended = (upsample(regions, up_weight) * full_mask[..., None]).astype(jnp.bfloat16)
        return refine(extended, full_mask, first_weight, second_weight)

    refined_all = lax.map(one_device, (jnp.arange(N_GRP, dtype=jnp.int32), ids_block, live_block))
    in_use_all = ids_block >= 0
    owner_onehot = ((owner_block[:, :, None] == jnp.arange(N_GRP, dtype=jnp.int32)[None, None, :]) & in_use_all[:, :, None]).astype(jnp.int32)
    earlier = jnp.cumsum(owner_onehot, axis=1) - owner_onehot
    owner_rank = jnp.sum(earlier * owner_onehot, axis=2)
    target = owner_block * OWN_ROWS + jnp.arange(N_GRP, dtype=jnp.int32)[:, None] * SCAP + owner_rank
    target = jnp.where(in_use_all, target, OUT_ROWS)
    flat_rows = refined_all.reshape(N_GRP * BPD, -1)
    result = jnp.zeros((OUT_ROWS, flat_rows.shape[1]), jnp.bfloat16).at[target.reshape(-1)].set(flat_rows, mode="drop")
    return result
```

```python
import jax
import jax.numpy as jnp
from jax import lax
from jax.experimental import pallas as pl
from jax.experimental.pallas import tpu as pltpu
from jax.sharding import PartitionSpec as P

G = 64
HB = 4
NB = 16
VMEM = pltpu.VMEM
SMEM = pltpu.SMEM
F32 = jnp.float32
BF16 = jnp.bfloat16


def conv_weights(w):
    z = jnp.zeros_like(w[:, :, :1])
    a = jnp.concatenate([jnp.concatenate([w, z], 2), jnp.concatenate([z, w], 2)], -1)
    z = jnp.zeros_like(a[:, :1])
    b = jnp.concatenate([jnp.concatenate([a, z], 1), jnp.concatenate([z, a], 1)], -1)
    return b.reshape(3, 1024, 256)


def up_weights(w):
    z = jnp.zeros_like(w[:, :, 0])
    a = jnp.stack(
        [jnp.concatenate([w[:, :, 1], w[:, :, 2]], -1), jnp.concatenate([z, w[:, :, 0]], -1)], 2
    )
    z = jnp.zeros_like(a[:, 0])
    b = jnp.stack(
        [jnp.concatenate([a[:, 1], a[:, 2]], -1), jnp.concatenate([z, a[:, 0]], -1)], 1
    )
    return b.reshape(3, 512, 256)


def gather_kernel(own_ids, prev_ids, next_ids, lat_ref, own_ref, down_ref, up_ref, pan, win):
    plane = pl.program_id(0)

    @pl.when(plane == 0)
    def _():
        pan[0] = jnp.zeros(pan.shape[1:], F32)
        pan[65:67] = jnp.zeros((2,) + pan.shape[1:], F32)
        pan[:, 0:8] = jnp.zeros((67, 8, 128), F32)
        pan[:, 72:80] = jnp.zeros((67, 8, 128), F32)

    pan[1:65, 8:72] = lat_ref[0].astype(F32)

    def gather(ids, out_ref):
        for b in range(NB):
            local = jnp.maximum(ids[b], 0)
            by = lax.rem(lax.div(local, 16), 16)
            bz = lax.rem(local, 16)
            for j in range(7):
                win[pl.ds((j * NB + b) * 8, 8), :] = pan[4 * by + j, pl.ds(4 * bz + 7, 8), :]
        for j in range(7):
            for l in range(7):
                out_ref[0, j, l] = win[pl.ds(j * 128 + l, 16, stride=8), :].astype(BF16)

    gather(own_ids, own_ref)

    @pl.when(plane < 2)
    def _():
        gather(prev_ids, down_ref)

    @pl.when(plane == 3)
    def _():
        gather(next_ids, up_ref)


def gather_regions(latents, own_ids, prev_ids, next_ids):
    smem = pl.BlockSpec(memory_space=SMEM)
    block = (1, 7, 7, NB, 128)
    return pl.pallas_call(
        gather_kernel,
        grid=(4,),
        in_specs=[smem, smem, smem, pl.BlockSpec((1, G, G, 128), lambda i: (i, 0, 0, 0))],
        out_specs=[
            pl.BlockSpec(block, lambda i: (i, 0, 0, 0, 0)),
            pl.BlockSpec(block, lambda i: (jnp.minimum(i, 1), 0, 0, 0, 0)),
            pl.BlockSpec(block, lambda i: (0, 0, 0, 0, 0)),
        ],
        out_shape=[
            jax.ShapeDtypeStruct((4, 7, 7, NB, 128), BF16),
            jax.ShapeDtypeStruct((2, 7, 7, NB, 128), BF16),
            jax.ShapeDtypeStruct((1, 7, 7, NB, 128), BF16),
        ],
        scratch_shapes=[VMEM((67, 80, 128), F32), VMEM((7 * NB * 8, 128), F32)],
        compiler_params=pltpu.CompilerParams(vmem_limit_bytes=32 << 20),
        name="gather_regions",
    )(own_ids, prev_ids, next_ids, latents)


def refine_kernel(
    inv, low_ref, own_ref, high_ref, live_ref, wu_ref, w1_ref, w2_ref, out_ref, reg, ext, hid, emask, hmask, fin
):
    reg[0:1] = low_ref[...]
    reg[1:5] = own_ref[...]
    reg[5:7] = high_ref[...]

    for n in range(27):
        emask[n // 9, n // 3 % 3, n % 3] = jnp.broadcast_to(live_ref[:, n : n + 1], (NB, 128))
    first = lax.broadcasted_iota(jnp.int32, (NB, 128), 1) < 64
    pair = ((0, 1), (1, 1), (1, 2))
    for cx in range(3):
        for cy in range(3):
            for cz in range(3):
                for py in range(2):
                    za, zb = pair[cz]
                    hmask[cx, cy, cz, py] = jnp.where(
                        first, emask[cx, pair[cy][py], za], emask[cx, pair[cy][py], zb]
                    )

    def spread(m, n):
        m = jnp.concatenate([m[0:1]] + [m[1:2]] * (n - 2) + [m[2:3]], 0)
        return jnp.concatenate([m[:, 0:1]] + [m[:, 1:2]] * (n - 2) + [m[:, 2:3]], 1)

    def dot(a, b):
        return jnp.dot(a, b, preferred_element_type=F32)

    def up_step(sub, _):
        def patch(i):
            return jnp.concatenate(
                [
                    reg[i, sy : sy + 6, sz : sz + 6].reshape(36 * NB, 128)
                    for sy in range(2)
                    for sz in range(2)
                ],
                1,
            )

        here, after = patch(sub), patch(sub + 1)
        even = dot(here, wu_ref[1])
        odd = dot(here, wu_ref[2]) + dot(after, wu_ref[0])
        cx = (sub >= 1).astype(jnp.int32) + (sub >= 5).astype(jnp.int32)
        m = spread(emask[cx], 6)
        for p, value in ((0, even), (1, odd)):
            for h in range(2):
                part = value[:, h * 128 : h * 128 + 128].reshape(6, 6, NB, 128)
                ext[2 * sub + p, :, :, h] = (part * m).astype(BF16)
        return 0

    lax.fori_loop(0, 6, up_step, 0)

    def conv(src, x, n, w_ref):
        total = None
        for kx in range(3):
            patch = jnp.concatenate(
                [
                    src[x + kx, dy : dy + n, dz : dz + n, qy].reshape(n * n * NB, 128)
                    for dy in range(2)
                    for qy in range(2)
                    for dz in range(2)
                ],
                1,
            )
            term = dot(patch, w_ref[kx])
            total = term if total is None else total + term
        return total

    def first_step(x, _):
        v = conv(ext, x, 5, w1_ref)
        v = (0.5 * v) * (1.0 + jnp.tanh(0.5 * v))
        cx = (x >= 1).astype(jnp.int32) + (x >= 9).astype(jnp.int32)
        m = hmask[cx]
        for h in range(2):
            part = v[:, h * 128 : h * 128 + 128].reshape(5, 5, NB, 128)
            hid[x, :, :, h] = (part * spread(m[:, :, h], 5)).astype(BF16)
        return 0

    lax.fori_loop(0, 10, first_step, 0)

    def second_step(x, _):
        v = conv(hid, x, 4, w2_ref)
        for py in range(2):
            part = v[:, py * 128 : py * 128 + 128].reshape(4, 4, NB, 128)
            part = part + ext[x + 2, 1:5, 1:5, py].astype(F32)
            for cy in range(4):
                fin[pl.ds((2 * cy + py) * 4 * NB, 4 * NB), :] = part[cy].reshape(4 * NB, 128)
        for s in range(32):
            b = jnp.maximum(inv[s], 0)
            used = inv[s] >= 0
            for g in range(2):
                rows = fin[pl.ds(g * 256 + b, 16, stride=NB), :]
                out_ref[s, pl.ds(pl.multiple_of(x * 32 + g * 16, 16), 16), :] = jnp.where(used, rows, 0.0).astype(BF16)
        return 0

    lax.fori_loop(0, 8, second_step, 0)


def refine_slots(inv, low, own, high, live, wu, w1, w2):
    vmem = pl.BlockSpec(memory_space=VMEM)
    return pl.pallas_call(
        refine_kernel,
        in_specs=[pl.BlockSpec(memory_space=SMEM)] + [vmem] * 7,
        out_specs=vmem,
        out_shape=jax.ShapeDtypeStruct((32, 256, 128), BF16),
        scratch_shapes=[
            VMEM((7, 7, 7, NB, 128), BF16),
            VMEM((12, 6, 6, 2, NB, 128), BF16),
            VMEM((10, 5, 5, 2, NB, 128), BF16),
            VMEM((3, 3, 3, NB, 128), F32),
            VMEM((3, 3, 3, 2, NB, 128), F32),
            VMEM((32 * NB, 128), F32),
        ],
        compiler_params=pltpu.CompilerParams(vmem_limit_bytes=48 << 20),
        name="refine_slots",
    )(inv, low, own, high, live, wu, w1, w2)


def live_flags(ids, neighbor_live, bricks_long, bricks_across):
    used = ids >= 0
    local = jnp.maximum(ids, 0)
    n = jnp.arange(27, dtype=jnp.int32)
    near_x = (lax.axis_index("grp") + local // (bricks_across * bricks_across))[:, None] + n // 9 - 1
    near_y = (local // bricks_across % bricks_across)[:, None] + n // 3 % 3 - 1
    near_z = (local % bricks_across)[:, None] + n % 3 - 1
    inside = (near_x >= 0) & (near_x < bricks_long)
    inside &= (near_y >= 0) & (near_y < bricks_across)
    inside &= (near_z >= 0) & (near_z < bricks_across)
    return (inside & ((neighbor_live > 0) | (n == 13)) & used[:, None]).astype(F32)


def slot_sources(ids, owner):
    used = ids >= 0
    r = jnp.arange(NB, dtype=jnp.int32)
    same = (owner[:, None] == owner[None, :]) & used[None, :] & (r[None, :] < r[:, None])
    slot = jnp.where(used, owner * 2 + jnp.sum(same.astype(jnp.int32), 1), -1)
    hit = slot[:, None] == jnp.arange(32, dtype=jnp.int32)[None, :]
    return jnp.sum(jnp.where(hit, r[:, None] + 1, 0), 0) - 1


def local(latents, up_weight, first_weight, second_weight, brick_ids, brick_owner, neighbor_live):
    count = lax.axis_size("grp")
    up = [(i, i + 1) for i in range(count - 1)]
    down = [(i + 1, i) for i in range(count - 1)]
    prev_ids = lax.ppermute(brick_ids, "grp", up)
    next_ids = lax.ppermute(brick_ids, "grp", down)
    own, to_prev, to_next = gather_regions(latents, brick_ids, prev_ids, next_ids)
    low = lax.ppermute(to_next, "grp", up)
    high = lax.ppermute(to_prev, "grp", down)
    live = live_flags(brick_ids, neighbor_live, count, G // HB)
    inv = slot_sources(brick_ids, brick_owner)
    slots = refine_slots(
        inv, low, own, high, live, up_weights(up_weight), conv_weights(first_weight), conv_weights(second_weight)
    )
    rows = lax.all_to_all(slots, "grp", split_axis=0, concat_axis=0, tiled=True)
    return rows.reshape(32, 32768)


def solution(mesh):
    rows = P(("shape", "grp"))
    in_specs = (rows, P(), P(), P(), rows, rows, rows)
    return jax.shard_map(local, mesh=mesh, in_specs=in_specs, out_specs=rows, check_vma=False)
```

```python
import jax
import jax.numpy as jnp
from jax import lax
from jax.experimental import pallas as pl
from jax.experimental.pallas import tpu as pltpu
from jax.sharding import PartitionSpec as P

G = 64
HB = 4
NB = 16
VMEM = pltpu.VMEM
SMEM = pltpu.SMEM
DMA = pltpu.SemaphoreType.DMA
F32 = jnp.float32
BF16 = jnp.bfloat16
MESH = pl.DeviceIdType.MESH

PEERS = sorted(
    ((dy, dx) for dy in range(4) for dx in range(4) if dy or dx),
    key=lambda s: -(min(s[0], 4 - s[0]) + min(s[1], 4 - s[1])),
)
UP_TAP = ((1, 2), (None, 0))
PHASES = (
    ((2, 5), (2, 7), ((1, 0), (1, 1), (2, 0), (2, 1), (3, 0), (3, 1), (4, 0))),
    ((0, 2), (0, 2), ((0, 0), (0, 1))),
    ((5, 8), (7, 10), ((4, 1), (5, 0), (5, 1))),
)


def kernel(
    ids,
    owner,
    lat_hbm,
    wu_hbm,
    w1_hbm,
    w2_hbm,
    near_ref,
    out_ref,
    lat,
    wu_raw,
    w1_raw,
    w2_raw,
    wu,
    w1,
    w2,
    pan,
    win,
    reg,
    to_prev,
    to_next,
    ext,
    hid,
    emask,
    hmask,
    fin,
    send,
    near_ids,
    inv,
    lat_sem,
    w_sem,
    id_send,
    id_recv,
    halo_send,
    halo_recv,
    own_sem,
    send_sem,
    recv_sem,
):
    count = lax.axis_size("grp")
    me = lax.axis_index("grp")
    row, col = me // 4, me % 4
    across = G // HB

    def peer(dy, dx):
        return (row + dy) % 4 * 4 + (col + dx) % 4

    barrier = pltpu.get_barrier_semaphore()
    for dy, dx in PEERS:
        pl.semaphore_signal(barrier, inc=1, device_id={"grp": peer(dy, dx)}, device_id_type=MESH)

    def lat_copy(p):
        return pltpu.make_async_copy(lat_hbm.at[p], lat.at[p], lat_sem.at[p])

    for p in range(4):
        lat_copy(p).start()
    w_copies = [
        pltpu.make_async_copy(s, d, w_sem.at[i])
        for i, (s, d) in enumerate(((wu_hbm, wu_raw), (w1_hbm, w1_raw), (w2_hbm, w2_raw)))
    ]
    for c in w_copies:
        c.start()

    slot = []
    for b in range(NB):
        rank = 0
        for r in range(b):
            rank = rank + jnp.where(owner[r] == owner[b], 1, 0)
        slot.append(jnp.where(ids[b] >= 0, owner[b] * 2 + rank, -1))
    for s in range(32):
        source = -1
        for b in range(NB):
            source = jnp.where(slot[b] == s, b, source)
        inv[s] = source

    entry = lax.broadcasted_iota(jnp.int32, (NB, 27), 0)
    n = lax.broadcasted_iota(jnp.int32, (NB, 27), 1)
    local = jnp.full((NB, 27), -1, jnp.int32)
    for b in range(NB):
        local = jnp.where(entry == b, ids[b], local)
    used = local >= 0
    local = jnp.maximum(local, 0)
    near_x = me + local // (across * across) + n // 9 - 1
    near_y = local // across % across + n // 3 % 3 - 1
    near_z = local % across + n % 3 - 1
    inside = (near_x >= 0) & (near_x < count) & (near_y >= 0) & (near_y < across)
    inside = inside & (near_z >= 0) & (near_z < across)
    live = jnp.where(inside & ((near_ref[...] > 0) | (n == 13)) & used, 1.0, 0.0)
    for k in range(27):
        emask[k // 9, k // 3 % 3, k % 3] = jnp.broadcast_to(live[:, k : k + 1], (NB, 128))
    first = lax.broadcasted_iota(jnp.int32, (NB, 128), 1) < 64
    pair = ((0, 1), (1, 1), (1, 2))
    for cx in range(3):
        for cy in range(3):
            for cz in range(3):
                for py in range(2):
                    za, zb = pair[cz]
                    hmask[cx, cy, cz, py] = jnp.where(
                        first, emask[cx, pair[cy][py], za], emask[cx, pair[cy][py], zb]
                    )

    pl.semaphore_wait(barrier, len(PEERS))
    id_up = pltpu.make_async_remote_copy(
        ids, near_ids.at[0], id_send.at[0], id_recv.at[0], device_id={"grp": me + 1}, device_id_type=MESH
    )
    id_down = pltpu.make_async_remote_copy(
        ids, near_ids.at[1], id_send.at[1], id_recv.at[1], device_id={"grp": me - 1}, device_id_type=MESH
    )

    @pl.when(me < count - 1)
    def _():
        id_up.start()

    @pl.when(me > 0)
    def _():
        id_down.start()

    def border(p, _):
        pan[p, 0] = jnp.zeros(pan.shape[2:], F32)
        pan[p, 65:67] = jnp.zeros((2,) + pan.shape[2:], F32)
        pan[p, :, 0:8] = jnp.zeros((67, 8, 128), F32)
        pan[p, :, 72:80] = jnp.zeros((67, 8, 128), F32)
        return 0

    lax.fori_loop(0, 4, border, 0)

    def gather(p, id_of, dst, q):
        def one(b, _):
            local = jnp.maximum(id_of(b), 0)
            by = local // across % across
            bz = local % across
            for j in range(7):
                win[pl.ds(pl.multiple_of((j * NB + b) * 8, 8), 8), :] = pan[p, 4 * by + j, pl.ds(4 * bz + 7, 8), :]
            return 0

        lax.fori_loop(0, NB, one, 0)

        def two(j, _):
            for l in range(7):
                dst[q, j, l] = win[pl.ds(j * 128 + l, NB, stride=8), :].astype(BF16)
            return 0

        lax.fori_loop(0, 7, two, 0)

    def plane_step(p, _):
        lat_copy(p).wait()
        pan[p, 1:65, 8:72] = lat[p].astype(F32)
        gather(p, lambda b: ids[b], reg, p + 1)
        return 0

    lax.fori_loop(0, 4, plane_step, 0)

    halo_up = pltpu.make_async_remote_copy(
        to_next, reg.at[pl.ds(0, 1)], halo_send.at[0], halo_recv.at[0], device_id={"grp": me + 1}, device_id_type=MESH
    )
    halo_down = pltpu.make_async_remote_copy(
        to_prev, reg.at[pl.ds(5, 2)], halo_send.at[1], halo_recv.at[1], device_id={"grp": me - 1}, device_id_type=MESH
    )

    @pl.when(me > 0)
    def _():
        id_up.wait_recv()
        gather(0, lambda b: near_ids[0, b], to_prev, 0)
        gather(1, lambda b: near_ids[0, b], to_prev, 1)
        halo_down.start()

    @pl.when(me < count - 1)
    def _():
        id_down.wait_recv()
        gather(3, lambda b: near_ids[1, b], to_next, 0)
        halo_up.start()

    for c in w_copies:
        c.wait()

    def wu_step(kx, _):
        for sy in range(2):
            for sz in range(2):
                parts = []
                for py in range(2):
                    for pz in range(2):
                        ky, kz = UP_TAP[sy][py], UP_TAP[sz][pz]
                        parts.append(
                            jnp.zeros((128, 64), BF16) if ky is None or kz is None else wu_raw[kx, ky, kz]
                        )
                at = (sy * 2 + sz) * 128
                wu[kx, at : at + 128] = jnp.concatenate(parts, 1)
        return 0

    lax.fori_loop(0, 3, wu_step, 0)

    def patch_weights(src, dst):
        def step(kx, _):
            zero = jnp.zeros((64, 64), BF16)

            def pick(ky, kz):
                return src[kx, ky, kz] if 0 <= ky < 3 and 0 <= kz < 3 else zero

            for ty in range(4):
                for tz in range(4):
                    parts = [pick(ty - py, tz - pz) for py in range(2) for pz in range(2)]
                    at = (ty * 4 + tz) * 64
                    dst[kx, at : at + 64] = jnp.concatenate(parts, 1)
            return 0

        lax.fori_loop(0, 3, step, 0)

    patch_weights(w1_raw, w1)
    patch_weights(w2_raw, w2)

    def spread(m, n):
        m = jnp.concatenate([m[0:1]] + [m[1:2]] * (n - 2) + [m[2:3]], 0)
        return jnp.concatenate([m[:, 0:1]] + [m[:, 1:2]] * (n - 2) + [m[:, 2:3]], 1)

    def dot(a, b):
        return jnp.dot(a, b, preferred_element_type=F32)

    def up_plane(sub, parity):
        def patch(i):
            return jnp.concatenate(
                [
                    reg[i, sy : sy + 6, sz : sz + 6].reshape(36 * NB, 128)
                    for sy in range(2)
                    for sz in range(2)
                ],
                1,
            )

        if parity:
            value = dot(patch(sub), wu[2]) + dot(patch(sub + 1), wu[0])
        else:
            value = dot(patch(sub), wu[1])
        m = spread(emask[(sub >= 1) + (sub >= 5)], 6)
        for h in range(2):
            part = value[:, h * 128 : h * 128 + 128].reshape(6, 6, NB, 128)
            ext[2 * sub + parity, :, :, h] = (part * m).astype(BF16)

    def conv(src, x, n, w_ref):
        total = None
        for kx in range(3):
            patch = jnp.concatenate(
                [
                    src[x + kx, dy : dy + n, dz : dz + n, qy].reshape(n * n * NB, 128)
                    for dy in range(2)
                    for qy in range(2)
                    for dz in range(2)
                ],
                1,
            )
            term = dot(patch, w_ref[kx])
            total = term if total is None else total + term
        return total

    def first_step(x, _):
        v = conv(ext, x, 5, w1)
        v = (0.5 * v) * (1.0 + jnp.tanh(0.5 * v))
        m = hmask[(x >= 1).astype(jnp.int32) + (x >= 9).astype(jnp.int32)]
        for h in range(2):
            part = v[:, h * 128 : h * 128 + 128].reshape(5, 5, NB, 128)
            hid[x, :, :, h] = (part * spread(m[:, :, h], 5)).astype(BF16)
        return 0

    def second_step(x, _):
        v = conv(hid, x, 4, w2)
        for py in range(2):
            part = v[:, py * 128 : py * 128 + 128].reshape(4, 4, NB, 128)
            part = part + ext[x + 2, 1:5, 1:5, py].astype(F32)
            for cy in range(4):
                fin[pl.ds((2 * cy + py) * 4 * NB, 4 * NB), :] = part[cy].reshape(4 * NB, 128)
        for s in range(32):
            b = jnp.maximum(inv[s], 0)
            filled = inv[s] >= 0
            for g in range(2):
                rows = fin[pl.ds(g * 256 + b, NB, stride=NB), :]
                at = pl.multiple_of(x * 32 + g * 16, 16)
                send[s, pl.ds(at, 16), :] = jnp.where(filled, rows, 0.0).astype(BF16)
        return 0

    copies = []
    for phase, ((x0, x1), (h0, h1), planes) in enumerate(PHASES):
        if phase == 1:

            @pl.when(me == 0)
            def _():
                reg[0] = jnp.zeros(reg.shape[1:], BF16)

            @pl.when(me > 0)
            def _():
                halo_up.wait_recv()

        if phase == 2:

            @pl.when(me == count - 1)
            def _():
                reg[5:7] = jnp.zeros((2,) + reg.shape[1:], BF16)

            @pl.when(me < count - 1)
            def _():
                halo_down.wait_recv()

        for sub, parity in planes:
            up_plane(sub, parity)
        lax.fori_loop(h0, h1, first_step, 0)
        lax.fori_loop(x0, x1, second_step, 0)
        cells = pl.ds(x0 * 32, (x1 - x0) * 32)
        own = pltpu.make_async_copy(
            send.at[pl.ds(2 * me, 2), cells], out_ref.at[pl.ds(2 * me, 2), cells], own_sem.at[phase]
        )
        for k, (dy, dx) in enumerate(PEERS):
            to = peer(dy, dx)
            c = pltpu.make_async_remote_copy(
                send.at[pl.ds(2 * to, 2), cells],
                out_ref.at[pl.ds(2 * me, 2), cells],
                send_sem.at[phase, k],
                recv_sem.at[phase, k],
                device_id={"grp": to},
                device_id_type=MESH,
            )
            c.start()
            copies.append(c)
        own.start()
        copies.append(own)

    @pl.when(me < count - 1)
    def _():
        id_up.wait_send()
        halo_up.wait_send()

    @pl.when(me > 0)
    def _():
        id_down.wait_send()
        halo_down.wait_send()

    for c in copies:
        c.wait()


def decode(ids, owner, latents, wu, w1, w2, near):
    smem = pl.BlockSpec(memory_space=SMEM)
    hbm = pl.BlockSpec(memory_space=pl.ANY)
    return pl.pallas_call(
        kernel,
        in_specs=[smem, smem, hbm, hbm, hbm, hbm, pl.BlockSpec(memory_space=VMEM)],
        out_specs=hbm,
        out_shape=jax.ShapeDtypeStruct((32, 256, 128), BF16),
        scratch_shapes=[
            VMEM((4, G, G, 128), BF16),
            VMEM((3, 3, 3, 128, 64), BF16),
            VMEM((3, 3, 3, 64, 64), BF16),
            VMEM((3, 3, 3, 64, 64), BF16),
            VMEM((3, 512, 256), BF16),
            VMEM((3, 1024, 256), BF16),
            VMEM((3, 1024, 256), BF16),
            VMEM((4, 67, 80, 128), F32),
            VMEM((7 * NB * 8, 128), F32),
            VMEM((7, 7, 7, NB, 128), BF16),
            VMEM((2, 7, 7, NB, 128), BF16),
            VMEM((1, 7, 7, NB, 128), BF16),
            VMEM((12, 6, 6, 2, NB, 128), BF16),
            VMEM((10, 5, 5, 2, NB, 128), BF16),
            VMEM((3, 3, 3, NB, 128), F32),
            VMEM((3, 3, 3, 2, NB, 128), F32),
            VMEM((32 * NB, 128), F32),
            VMEM((32, 256, 128), BF16),
            SMEM((2, NB), jnp.int32),
            SMEM((32,), jnp.int32),
            DMA((4,)),
            DMA((3,)),
            DMA((2,)),
            DMA((2,)),
            DMA((2,)),
            DMA((2,)),
            DMA((3,)),
            DMA((3, 15)),
            DMA((3, 15)),
        ],
        compiler_params=pltpu.CompilerParams(
            collective_id=0, has_side_effects=True, vmem_limit_bytes=56 << 20
        ),
        name="decode",
    )(ids, owner, latents, wu, w1, w2, near)


def local(latents, up_weight, first_weight, second_weight, brick_ids, brick_owner, neighbor_live):
    rows = decode(brick_ids, brick_owner, latents, up_weight, first_weight, second_weight, neighbor_live)
    return rows.reshape(32, 32768)


def solution(mesh):
    rows = P(("shape", "grp"))
    in_specs = (rows, P(), P(), P(), rows, rows, rows)
    return jax.shard_map(local, mesh=mesh, in_specs=in_specs, out_specs=rows, check_vma=False)
```

```python
import jax
import jax.numpy as jnp
from jax import lax
from jax.experimental import pallas as pl
from jax.experimental.pallas import tpu as pltpu
from jax.sharding import PartitionSpec as P

G = 64
HB = 4
NB = 16
VMEM = pltpu.VMEM
SMEM = pltpu.SMEM
DMA = pltpu.SemaphoreType.DMA
F32 = jnp.float32
BF16 = jnp.bfloat16
MESH = pl.DeviceIdType.MESH

PEERS = sorted(
    ((dy, dx) for dy in range(4) for dx in range(4) if dy or dx),
    key=lambda s: -(min(s[0], 4 - s[0]) + min(s[1], 4 - s[1])),
)
UP_TAP = ((1, 2), (None, 0))
def kernel(
    ids,
    owner,
    lat_hbm,
    wu_hbm,
    w1_hbm,
    w2_hbm,
    near_ref,
    out_ref,
    lat,
    wu_raw,
    w1_raw,
    w2_raw,
    wu,
    w1,
    w2,
    pan,
    win,
    reg,
    to_prev,
    to_next,
    ext,
    hid,
    emask,
    hmask,
    pick,
    send,
    near_ids,
    lat_sem,
    w_sem,
    id_send,
    id_recv,
    halo_send,
    halo_recv,
    own_sem,
    send_sem,
    recv_sem,
):
    count = lax.axis_size("grp")
    me = lax.axis_index("grp")
    row, col = me // 4, me % 4
    across = G // HB

    def peer(dy, dx):
        return (row + dy) % 4 * 4 + (col + dx) % 4

    barrier = pltpu.get_barrier_semaphore()
    for dy, dx in PEERS:
        pl.semaphore_signal(barrier, inc=1, device_id={"grp": peer(dy, dx)}, device_id_type=MESH)

    def lat_copy(p):
        return pltpu.make_async_copy(lat_hbm.at[p], lat.at[p], lat_sem.at[p])

    for p in range(4):
        lat_copy(p).start()
    w_copies = [
        pltpu.make_async_copy(s, d, w_sem.at[i])
        for i, (s, d) in enumerate(((wu_hbm, wu_raw), (w1_hbm, w1_raw), (w2_hbm, w2_raw)))
    ]
    for c in w_copies:
        c.start()

    col_id = lax.broadcasted_iota(jnp.int32, (512, 256), 1)
    row_id = lax.broadcasted_iota(jnp.int32, (512, 256), 0)
    slot = jnp.full((1, 256), -1, jnp.int32)
    entry = lax.broadcasted_iota(jnp.int32, (1, 256), 1) % NB
    for b in range(NB):
        rank = 0
        for r in range(b):
            rank = rank + jnp.where(owner[r] == owner[b], 1, 0)
        slot = jnp.where(entry == b, jnp.where(ids[b] >= 0, owner[b] * 2 + rank, -1), slot)
    hit = (row_id // NB == slot) & (row_id % NB == col_id // NB)
    pick[...] = jnp.where(hit, 1.0, 0.0).astype(BF16)

    entry = lax.broadcasted_iota(jnp.int32, (NB, 27), 0)
    n = lax.broadcasted_iota(jnp.int32, (NB, 27), 1)
    local = jnp.full((NB, 27), -1, jnp.int32)
    for b in range(NB):
        local = jnp.where(entry == b, ids[b], local)
    used = local >= 0
    local = jnp.maximum(local, 0)
    near_x = me + local // (across * across) + n // 9 - 1
    near_y = local // across % across + n // 3 % 3 - 1
    near_z = local % across + n % 3 - 1
    inside = (near_x >= 0) & (near_x < count) & (near_y >= 0) & (near_y < across)
    inside = inside & (near_z >= 0) & (near_z < across)
    live = jnp.where(inside & ((near_ref[...] > 0) | (n == 13)) & used, 1.0, 0.0)
    for k in range(27):
        emask[k // 9, k // 3 % 3, k % 3] = jnp.broadcast_to(live[:, k : k + 1], (NB, 128))
    first = lax.broadcasted_iota(jnp.int32, (NB, 128), 1) < 64
    pair = ((0, 1), (1, 1), (1, 2))
    for cx in range(3):
        for cy in range(3):
            for cz in range(3):
                for py in range(2):
                    za, zb = pair[cz]
                    hmask[cx, cy, cz, py] = jnp.where(
                        first, emask[cx, pair[cy][py], za], emask[cx, pair[cy][py], zb]
                    )

    for c in w_copies:
        c.wait()

    def wu_step(kx, _):
        for sy in range(2):
            for sz in range(2):
                parts = []
                for py in range(2):
                    for pz in range(2):
                        ky, kz = UP_TAP[sy][py], UP_TAP[sz][pz]
                        parts.append(
                            jnp.zeros((64, 128), BF16) if ky is None or kz is None else wu_raw[kx, ky, kz]
                        )
                at = (sy * 2 + sz) * 128
                wu[kx, :, at : at + 128] = jnp.concatenate(parts, 0)
        return 0

    lax.fori_loop(0, 3, wu_step, 0)

    def patch_weights(src, dst):
        def step(kx, _):
            zero = jnp.zeros((64, 64), BF16)

            def pick(ky, kz):
                return src[kx, ky, kz] if 0 <= ky < 3 and 0 <= kz < 3 else zero

            for ty in range(4):
                for tz in range(4):
                    parts = [pick(ty - py, tz - pz) for py in range(2) for pz in range(2)]
                    at = (ty * 4 + tz) * 64
                    dst[kx, at : at + 64] = jnp.concatenate(parts, 1)
            return 0

        lax.fori_loop(0, 3, step, 0)

    patch_weights(w1_raw, w1)
    patch_weights(w2_raw, w2)

    pl.semaphore_wait(barrier, len(PEERS))
    id_up = pltpu.make_async_remote_copy(
        ids, near_ids.at[0], id_send.at[0], id_recv.at[0], device_id={"grp": me + 1}, device_id_type=MESH
    )
    id_down = pltpu.make_async_remote_copy(
        ids, near_ids.at[1], id_send.at[1], id_recv.at[1], device_id={"grp": me - 1}, device_id_type=MESH
    )

    @pl.when(me < count - 1)
    def _():
        id_up.start()

    @pl.when(me > 0)
    def _():
        id_down.start()

    def border(p, _):
        pan[p, 0] = jnp.zeros(pan.shape[2:], F32)
        pan[p, 65:67] = jnp.zeros((2,) + pan.shape[2:], F32)
        pan[p, :, 0:8] = jnp.zeros((67, 8, 128), F32)
        pan[p, :, 72:80] = jnp.zeros((67, 8, 128), F32)
        return 0

    lax.fori_loop(0, 4, border, 0)

    def gather(p, id_of, dst, q):
        def one(b, _):
            local = jnp.maximum(id_of(b), 0)
            by = local // across % across
            bz = local % across
            for j in range(7):
                win[pl.ds(pl.multiple_of((j * NB + b) * 8, 8), 8), :] = pan[p, 4 * by + j, pl.ds(4 * bz + 7, 8), :]
            return 0

        lax.fori_loop(0, NB, one, 0)

        def two(j, _):
            for l in range(7):
                dst[q, j, l] = win[pl.ds(j * 128 + l, NB, stride=8), :].astype(BF16)
            return 0

        lax.fori_loop(0, 7, two, 0)

    def plane_step(p, _):
        lat_copy(p).wait()
        pan[p, 1:65, 8:72] = lat[p].astype(F32)
        gather(p, lambda b: ids[b], reg, p + 1)
        return 0

    lax.fori_loop(0, 4, plane_step, 0)

    halo_up = pltpu.make_async_remote_copy(
        to_next, reg.at[pl.ds(0, 1)], halo_send.at[0], halo_recv.at[0], device_id={"grp": me + 1}, device_id_type=MESH
    )
    halo_down = pltpu.make_async_remote_copy(
        to_prev, reg.at[pl.ds(5, 2)], halo_send.at[1], halo_recv.at[1], device_id={"grp": me - 1}, device_id_type=MESH
    )

    @pl.when(me > 0)
    def _():
        id_up.wait_recv()
        gather(0, lambda b: near_ids[0, b], to_prev, 0)
        gather(1, lambda b: near_ids[0, b], to_prev, 1)
        halo_down.start()

    @pl.when(me < count - 1)
    def _():
        id_down.wait_recv()
        gather(3, lambda b: near_ids[1, b], to_next, 0)
        halo_up.start()

    def spread(m, n):
        m = jnp.concatenate([m[0:1]] + [m[1:2]] * (n - 2) + [m[2:3]], 0)
        return jnp.concatenate([m[:, 0:1]] + [m[:, 1:2]] * (n - 2) + [m[:, 2:3]], 1)

    def dot(a, b):
        return jnp.dot(a, b, preferred_element_type=F32)

    def dot_t(a, b):
        return lax.dot_general(a, b, (((1,), (1,)), ((), ())), preferred_element_type=F32)

    def up_plane(e):
        sub = e // 2

        def patch(i):
            return jnp.concatenate(
                [
                    reg[i, sy : sy + 6, sz : sz + 6].reshape(36 * NB, 128)
                    for sy in range(2)
                    for sz in range(2)
                ],
                1,
            )

        def put(value):
            m = spread(emask[(e >= 2).astype(jnp.int32) + (e >= 10).astype(jnp.int32)], 6)
            for h in range(2):
                part = value[:, h * 128 : h * 128 + 128].reshape(6, 6, NB, 128)
                ext[e, :, :, h] = (part * m).astype(BF16)

        @pl.when(e % 2 == 0)
        def _():
            put(dot_t(patch(sub), wu[1]))

        @pl.when(e % 2 == 1)
        def _():
            put(dot_t(patch(sub), wu[2]) + dot_t(patch(sub + 1), wu[0]))

    def conv(src, x, n, w_ref):
        total = None
        for kx in range(3):
            patch = jnp.concatenate(
                [
                    src[x + kx, dy : dy + n, dz : dz + n, qy].reshape(n * n * NB, 128)
                    for dy in range(2)
                    for qy in range(2)
                    for dz in range(2)
                ],
                1,
            )
            term = dot(patch, w_ref[kx])
            total = term if total is None else total + term
        return total

    def first_plane(x):
        v = conv(ext, x, 5, w1)
        v = (0.5 * v) * (1.0 + jnp.tanh(0.5 * v))
        m = hmask[(x >= 1).astype(jnp.int32) + (x >= 9).astype(jnp.int32)]
        for h in range(2):
            part = v[:, h * 128 : h * 128 + 128].reshape(5, 5, NB, 128)
            hid[x, :, :, h] = (part * spread(m[:, :, h], 5)).astype(BF16)

    def second_plane(x):
        v = conv(hid, x, 4, w2)
        own = [ext[x + 2, 1:5, 1:5, h].reshape(16 * NB, 128) for h in range(2)]
        v = (v + jnp.concatenate(own, 1).astype(F32)).astype(BF16)
        placed = dot(pick[...], v).astype(BF16)
        for h in range(2):
            send[:, x, h] = placed[:, h * 128 : h * 128 + 128].reshape(32, NB, 128)

    def plane_copy(k, x):
        dy, dx = PEERS[k]
        to = peer(dy, dx)
        return pltpu.make_async_remote_copy(
            send.at[pl.ds(2 * to, 2), x],
            out_ref.at[pl.ds(2 * me, 2), x],
            send_sem.at[k],
            recv_sem.at[k],
            device_id={"grp": to},
            device_id_type=MESH,
        )

    up_plane(jnp.int32(2))
    up_plane(jnp.int32(3))

    def step(t, _):
        h = jnp.where(t < 5, t + 2, jnp.where(t < 7, 6 - t, t))
        x = jnp.where(t < 5, h - 2, jnp.where(t < 7, h, h - 2))

        @pl.when((t == 5) & (me == 0))
        def _():
            reg[0] = jnp.zeros(reg.shape[1:], BF16)

        @pl.when((t == 5) & (me > 0))
        def _():
            halo_up.wait_recv()

        @pl.when((t == 7) & (me == count - 1))
        def _():
            reg[5:7] = jnp.zeros((2,) + reg.shape[1:], BF16)

        @pl.when((t == 7) & (me < count - 1))
        def _():
            halo_down.wait_recv()

        up_plane(jnp.where(t < 5, h + 2, jnp.where(t < 7, h, h + 2)))
        first_plane(h)

        @pl.when(t >= 2)
        def _():
            second_plane(x)
            for k in range(len(PEERS)):
                plane_copy(k, x).start()

        return 0

    lax.fori_loop(0, 10, step, 0)

    own = pltpu.make_async_copy(send.at[pl.ds(2 * me, 2)], out_ref.at[pl.ds(2 * me, 2)], own_sem.at[0])
    own.start()

    @pl.when(me < count - 1)
    def _():
        id_up.wait_send()
        halo_up.wait_send()

    @pl.when(me > 0)
    def _():
        id_down.wait_send()
        halo_down.wait_send()

    own.wait()
    for k, (dy, dx) in enumerate(PEERS):
        to = peer(dy, dx)
        pltpu.make_async_remote_copy(
            send.at[pl.ds(2 * to, 2)],
            out_ref.at[pl.ds(2 * me, 2)],
            send_sem.at[k],
            recv_sem.at[k],
            device_id={"grp": to},
            device_id_type=MESH,
        ).wait()


def decode(ids, owner, latents, wu, w1, w2, near):
    smem = pl.BlockSpec(memory_space=SMEM)
    hbm = pl.BlockSpec(memory_space=pl.ANY)
    return pl.pallas_call(
        kernel,
        in_specs=[smem, smem, hbm, hbm, hbm, hbm, pl.BlockSpec(memory_space=VMEM)],
        out_specs=hbm,
        out_shape=jax.ShapeDtypeStruct((32, 8, 2, NB, 128), BF16),
        scratch_shapes=[
            VMEM((4, G, G, 128), BF16),
            VMEM((3, 3, 3, 64, 128), BF16),
            VMEM((3, 3, 3, 64, 64), BF16),
            VMEM((3, 3, 3, 64, 64), BF16),
            VMEM((3, 256, 512), BF16),
            VMEM((3, 1024, 256), BF16),
            VMEM((3, 1024, 256), BF16),
            VMEM((4, 67, 80, 128), F32),
            VMEM((7 * NB * 8, 128), F32),
            VMEM((7, 7, 7, NB, 128), BF16),
            VMEM((2, 7, 7, NB, 128), BF16),
            VMEM((1, 7, 7, NB, 128), BF16),
            VMEM((12, 6, 6, 2, NB, 128), BF16),
            VMEM((10, 5, 5, 2, NB, 128), BF16),
            VMEM((3, 3, 3, NB, 128), F32),
            VMEM((3, 3, 3, 2, NB, 128), F32),
            VMEM((512, 256), BF16),
            VMEM((32, 8, 2, NB, 128), BF16),
            SMEM((2, NB), jnp.int32),
            DMA((4,)),
            DMA((3,)),
            DMA((2,)),
            DMA((2,)),
            DMA((2,)),
            DMA((2,)),
            DMA((1,)),
            DMA((15,)),
            DMA((15,)),
        ],
        compiler_params=pltpu.CompilerParams(
            collective_id=0, has_side_effects=True, vmem_limit_bytes=56 << 20
        ),
        name="decode",
    )(ids, owner, latents, wu, w1, w2, near)


def order_kernel(in_ref, out_ref, turn):
    @pl.when(pl.program_id(0) == 0)
    def _():
        i = lax.broadcasted_iota(jnp.int32, (256, 256), 0)
        j = lax.broadcasted_iota(jnp.int32, (256, 256), 1)
        hit = (i // 8 % NB == j % NB) & (i // 128 * 8 + i % 8 == j // NB)
        turn[...] = jnp.where(hit, 1.0, 0.0).astype(BF16)

    for half in range(2):
        rows = [in_ref[half * 16 : half * 16 + 16, 0, h].reshape(256, 128) for h in range(2)]
        v = jnp.dot(turn[...], jnp.concatenate(rows, 1), preferred_element_type=F32).astype(BF16)
        for block in range(2):
            for cy in range(4):
                for h in range(2):
                    at = block * 128 + cy * 32
                    to = (2 * cy + h) * 32
                    out_ref[2 * half + block, to : to + 32] = v[at : at + 32, h * 128 : h * 128 + 128]


def ordered(rows):
    out = pl.pallas_call(
        order_kernel,
        grid=(8,),
        in_specs=[pl.BlockSpec((32, 1, 2, NB, 128), lambda i: (0, i, 0, 0, 0))],
        out_specs=pl.BlockSpec((4, 256, 128), lambda i: (0, i, 0)),
        out_shape=jax.ShapeDtypeStruct((4, 2048, 128), BF16),
        scratch_shapes=[VMEM((256, 256), BF16)],
        name="order",
    )(rows)
    return out.reshape(4, 256, 8, 128).transpose(0, 2, 1, 3).reshape(32, 32768)


def local(latents, up_weight, first_weight, second_weight, brick_ids, brick_owner, neighbor_live):
    turned = jnp.swapaxes(up_weight, 3, 4)
    rows = decode(brick_ids, brick_owner, latents, turned, first_weight, second_weight, neighbor_live)
    return ordered(rows)


def solution(mesh):
    rows = P(("shape", "grp"))
    in_specs = (rows, P(), P(), P(), rows, rows, rows)
    return jax.shard_map(local, mesh=mesh, in_specs=in_specs, out_specs=rows, check_vma=False)
```

```python
import jax
import jax.numpy as jnp
from jax import lax
from jax.experimental import pallas as pl
from jax.experimental.pallas import tpu as pltpu
from jax.sharding import PartitionSpec as P

G = 64
HB = 4
NB = 16
VMEM = pltpu.VMEM
SMEM = pltpu.SMEM
DMA = pltpu.SemaphoreType.DMA
F32 = jnp.float32
BF16 = jnp.bfloat16
MESH = pl.DeviceIdType.MESH

PEERS = sorted(
    ((dy, dx) for dy in range(4) for dx in range(4) if dy or dx),
    key=lambda s: -(min(s[0], 4 - s[0]) + min(s[1], 4 - s[1])),
)
UP_TAP = ((1, 2), (None, 0))
EXT_ORDER = (2, 3, 4, 5, 6, 7, 8, 1, 0, 9, 10, 11)
HID_ORDER = (2, 3, 4, 5, 6, 1, 0, 7, 8, 9)
OUT_ORDER = (2, 3, 4, 1, 0, 5, 6, 7)


def kernel(
    ids,
    owner,
    lat_hbm,
    wu_hbm,
    w1_hbm,
    w2_hbm,
    near_ref,
    out_ref,
    lat,
    wu_raw,
    w1_raw,
    w2_raw,
    wu,
    w1,
    w2,
    pan,
    win,
    reg,
    to_prev,
    to_next,
    ext,
    hid,
    emask,
    hmask,
    pick,
    turn,
    done,
    send,
    recv,
    stage,
    near_ids,
    lat_sem,
    w_sem,
    id_send,
    id_recv,
    halo_send,
    halo_recv,
    own_sem,
    out_sem,
    send_sem,
    recv_sem,
):
    count = lax.axis_size("grp")
    me = lax.axis_index("grp")
    row, col = me // 4, me % 4
    after, before = (me + 1) % count, (me + count - 1) % count
    across = G // HB

    def peer(dy, dx):
        return (row + dy) % 4 * 4 + (col + dx) % 4

    barrier = pltpu.get_barrier_semaphore()
    for dy, dx in PEERS:
        pl.semaphore_signal(barrier, inc=1, device_id={"grp": peer(dy, dx)}, device_id_type=MESH)

    def lat_copy(p):
        return pltpu.make_async_copy(lat_hbm.at[p], lat.at[p], lat_sem.at[p])

    w_copies = [
        pltpu.make_async_copy(s, d, w_sem.at[i])
        for i, (s, d) in enumerate(((wu_hbm, wu_raw), (w1_hbm, w1_raw), (w2_hbm, w2_raw)))
    ]
    for p in (0, 1, 3):
        lat_copy(p).start()
    w_copies[0].start()
    w_copies[1].start()
    lat_copy(2).start()
    w_copies[2].start()

    def border(p, _):
        pan[p, 0] = jnp.zeros(pan.shape[2:], F32)
        pan[p, 65:67] = jnp.zeros((2,) + pan.shape[2:], F32)
        pan[p, :, 0:8] = jnp.zeros((67, 8, 128), F32)
        pan[p, :, 72:80] = jnp.zeros((67, 8, 128), F32)
        return 0

    lax.fori_loop(0, 4, border, 0)

    def load_plane(p):
        lat_copy(p).wait()
        pan[p, 1:65, 8:72] = lat[p].astype(F32)

    def gather(p, id_of, dst, q):
        def one(b, _):
            local = jnp.maximum(id_of(b), 0)
            by = local // across % across
            bz = local % across
            for j in range(7):
                win[pl.ds(pl.multiple_of((j * NB + b) * 8, 8), 8), :] = pan[p, 4 * by + j, pl.ds(4 * bz + 7, 8), :]
            return 0

        lax.fori_loop(0, NB, one, 0)

        def two(j, _):
            for l in range(7):
                dst[q, j, l] = win[pl.ds(j * 128 + l, NB, stride=8), :].astype(BF16)
            return 0

        lax.fori_loop(0, 7, two, 0)

    pl.semaphore_wait(barrier, len(PEERS))
    id_up = pltpu.make_async_remote_copy(
        ids, near_ids.at[0], id_send.at[0], id_recv.at[0], device_id={"grp": after}, device_id_type=MESH
    )
    id_down = pltpu.make_async_remote_copy(
        ids, near_ids.at[1], id_send.at[1], id_recv.at[1], device_id={"grp": before}, device_id_type=MESH
    )
    id_up.start()
    id_down.start()

    halo_up = pltpu.make_async_remote_copy(
        to_next, reg.at[pl.ds(0, 1)], halo_send.at[0], halo_recv.at[0], device_id={"grp": after}, device_id_type=MESH
    )
    halo_down = [
        pltpu.make_async_remote_copy(
            to_prev.at[i],
            reg.at[5 + i],
            halo_send.at[1 + i],
            halo_recv.at[1 + i],
            device_id={"grp": before},
            device_id_type=MESH,
        )
        for i in range(2)
    ]
    load_plane(0)
    gather(0, lambda b: ids[b], reg, 1)
    load_plane(1)
    id_up.wait()
    for p in range(2):
        gather(p, lambda b: near_ids[0, b], to_prev, p)
        halo_down[p].start()
    load_plane(3)
    id_down.wait()
    gather(3, lambda b: near_ids[1, b], to_next, 0)
    halo_up.start()
    gather(1, lambda b: ids[b], reg, 2)
    load_plane(2)
    gather(2, lambda b: ids[b], reg, 3)

    entry = lax.broadcasted_iota(jnp.int32, (NB, 27), 0)
    n = lax.broadcasted_iota(jnp.int32, (NB, 27), 1)
    local = jnp.full((NB, 27), -1, jnp.int32)
    for b in range(NB):
        local = jnp.where(entry == b, ids[b], local)
    used = local >= 0
    local = jnp.maximum(local, 0)
    near_x = me + local // (across * across) + n // 9 - 1
    near_y = local // across % across + n // 3 % 3 - 1
    near_z = local % across + n % 3 - 1
    inside = (near_x >= 0) & (near_x < count) & (near_y >= 0) & (near_y < across)
    inside = inside & (near_z >= 0) & (near_z < across)
    live = jnp.where(inside & ((near_ref[...] > 0) | (n == 13)) & used, 1.0, 0.0)
    for k in range(27):
        emask[k // 9, k // 3 % 3, k % 3] = jnp.broadcast_to(live[:, k : k + 1], (NB, 128))
    first = lax.broadcasted_iota(jnp.int32, (NB, 128), 1) < 64
    pair = ((0, 1), (1, 1), (1, 2))
    for cx in range(3):
        for cy in range(3):
            for cz in range(3):
                for py in range(2):
                    za, zb = pair[cz]
                    hmask[cx, cy, cz, py] = jnp.where(
                        first, emask[cx, pair[cy][py], za], emask[cx, pair[cy][py], zb]
                    )

    w_copies[0].wait()

    def wu_step(kx, _):
        for sy in range(2):
            for sz in range(2):
                parts = []
                for py in range(2):
                    for pz in range(2):
                        ky, kz = UP_TAP[sy][py], UP_TAP[sz][pz]
                        parts.append(
                            jnp.zeros((64, 128), BF16) if ky is None or kz is None else wu_raw[kx, ky, kz]
                        )
                at = (sy * 2 + sz) * 128
                wu[kx, at : at + 128] = jnp.concatenate(parts, 0).T
        return 0

    lax.fori_loop(0, 3, wu_step, 0)

    def patch_weights(src, dst):
        def step(kx, _):
            zero = jnp.zeros((64, 64), BF16)

            def pick(ky, kz):
                return src[kx, ky, kz] if 0 <= ky < 3 and 0 <= kz < 3 else zero

            for ty in range(4):
                for tz in range(4):
                    parts = [pick(ty - py, tz - pz) for py in range(2) for pz in range(2)]
                    at = (ty * 4 + tz) * 64
                    dst[kx, at : at + 64] = jnp.concatenate(parts, 1)
            return 0

        lax.fori_loop(0, 3, step, 0)

    w_copies[1].wait()
    patch_weights(w1_raw, w1)
    w_copies[2].wait()
    patch_weights(w2_raw, w2)

    col_id = lax.broadcasted_iota(jnp.int32, (512, 256), 1)
    row_id = lax.broadcasted_iota(jnp.int32, (512, 256), 0)
    slot = jnp.full((1, 256), -1, jnp.int32)
    entry = lax.broadcasted_iota(jnp.int32, (1, 256), 1) % NB
    for b in range(NB):
        rank = 0
        for r in range(b):
            rank = rank + jnp.where(owner[r] == owner[b], 1, 0)
        slot = jnp.where(entry == b, jnp.where(ids[b] >= 0, owner[b] * 2 + rank, -1), slot)
    hit = (row_id // NB == slot) & (row_id % NB == col_id // NB)
    pick[...] = jnp.where(hit, 1.0, 0.0).astype(BF16)

    def spread(m, n):
        m = jnp.concatenate([m[0:1]] + [m[1:2]] * (n - 2) + [m[2:3]], 0)
        return jnp.concatenate([m[:, 0:1]] + [m[:, 1:2]] * (n - 2) + [m[:, 2:3]], 1)

    def dot(a, b):
        return jnp.dot(a, b, preferred_element_type=F32)

    def up_plane(e):
        sub = e // 2

        def patch(i):
            return jnp.concatenate(
                [
                    reg[i, sy : sy + 6, sz : sz + 6].reshape(36 * NB, 128)
                    for sy in range(2)
                    for sz in range(2)
                ],
                1,
            )

        if e % 2:
            value = dot(patch(sub), wu[2]) + dot(patch(sub + 1), wu[0])
        else:
            value = dot(patch(sub), wu[1])
        m = spread(emask[(e >= 2) + (e >= 10)], 6)
        for h in range(2):
            part = value[:, h * 128 : h * 128 + 128].reshape(6, 6, NB, 128)
            ext[e, :, :, h] = (part * m).astype(BF16)

    def conv(src, x, n, w_ref):
        total = None
        for kx in range(3):
            patch = jnp.concatenate(
                [
                    src[x + kx, dy : dy + n, dz : dz + n, qy].reshape(n * n * NB, 128)
                    for dy in range(2)
                    for qy in range(2)
                    for dz in range(2)
                ],
                1,
            )
            term = dot(patch, w_ref[kx])
            total = term if total is None else total + term
        return total

    def first_plane(x):
        v = conv(ext, x, 5, w1)
        v = (0.5 * v) * (1.0 + jnp.tanh(0.5 * v))
        m = hmask[(x >= 1) + (x >= 9)]
        for h in range(2):
            part = v[:, h * 128 : h * 128 + 128].reshape(5, 5, NB, 128)
            hid[x, :, :, h] = (part * spread(m[:, :, h], 5)).astype(BF16)

    def second_plane(x):
        v = conv(hid, x, 4, w2)
        own = [ext[x + 2, 1:5, 1:5, h].reshape(16 * NB, 128) for h in range(2)]
        done[x] = (v + jnp.concatenate(own, 1).astype(F32)).astype(BF16)

    def plane_copy(k, x):
        dy, dx = PEERS[k]
        to = peer(dy, dx)
        return pltpu.make_async_remote_copy(
            send.at[x, pl.ds(2 * to, 2)],
            recv.at[x, pl.ds(2 * me, 2)],
            send_sem.at[x, k],
            recv_sem.at[x, k],
            device_id={"grp": to},
            device_id_type=MESH,
        )

    def own_copy(x):
        return pltpu.make_async_copy(send.at[x, pl.ds(2 * me, 2)], recv.at[x, pl.ds(2 * me, 2)], own_sem.at[x])

    def send_plane(x):
        placed = dot(pick[...], done[x]).astype(BF16)
        for h in range(2):
            send[x, :, h] = placed[:, h * 128 : h * 128 + 128].reshape(32, NB, 128)
        for k in range(len(PEERS)):
            plane_copy(k, x).start()
        own_copy(x).start()

    for e in EXT_ORDER[:3]:
        up_plane(e)

    for t in range(10):
        first_plane(HID_ORDER[t])
        if t >= 2:
            second_plane(OUT_ORDER[t - 2])
            send_plane(OUT_ORDER[t - 2])
        if t + 3 < 12:
            e = EXT_ORDER[t + 3]
            if e == 7:
                gather(3, lambda b: ids[b], reg, 4)
            if e == 1:
                halo_up.wait_recv()
            if e == 9:
                for c in halo_down:
                    c.wait_recv()

                @pl.when(me == count - 1)
                def _():
                    reg[5:7] = jnp.zeros((2,) + reg.shape[1:], BF16)

            up_plane(e)

    i = lax.broadcasted_iota(jnp.int32, (256, 256), 0)
    j = lax.broadcasted_iota(jnp.int32, (256, 256), 1)
    hit = (i // 8 % NB == j % NB) & (i // 128 * 8 + i % 8 == j // NB)
    turn[...] = jnp.where(hit, 1.0, 0.0).astype(BF16)

    def out_copy(x):
        cells = pl.ds(x * 256, 256)
        return pltpu.make_async_copy(stage.at[:, cells], out_ref.at[:, cells], out_sem.at[x])

    def arrive(n, _):
        x = jnp.where(n < 3, n + 2, jnp.where(n < 5, 4 - n, n))
        own_copy(x).wait()
        for k in range(len(PEERS)):
            plane_copy(k, x).wait()
        for half in range(2):
            rows = [recv[x, half * 16 : half * 16 + 16, h].reshape(256, 128) for h in range(2)]
            v = dot(turn[...], jnp.concatenate(rows, 1)).astype(BF16)
            for block in range(2):
                for cy in range(4):
                    for h in range(2):
                        at = block * 128 + cy * 32
                        to = pl.multiple_of(x * 256 + (2 * cy + h) * 32, 32)
                        stage[2 * half + block, pl.ds(to, 32)] = v[at : at + 32, h * 128 : h * 128 + 128]
        out_copy(x).start()
        return 0

    lax.fori_loop(0, 8, arrive, 0)
    halo_up.wait_send()
    for c in halo_down:
        c.wait_send()
    for x in range(8):
        out_copy(x).wait()


def decode(ids, owner, latents, wu, w1, w2, near):
    smem = pl.BlockSpec(memory_space=SMEM)
    hbm = pl.BlockSpec(memory_space=pl.ANY)
    return pl.pallas_call(
        kernel,
        in_specs=[smem, smem, hbm, hbm, hbm, hbm, pl.BlockSpec(memory_space=VMEM)],
        out_specs=hbm,
        out_shape=jax.ShapeDtypeStruct((4, 2048, 128), BF16),
        scratch_shapes=[
            VMEM((4, G, G, 128), BF16),
            VMEM((3, 3, 3, 64, 128), BF16),
            VMEM((3, 3, 3, 64, 64), BF16),
            VMEM((3, 3, 3, 64, 64), BF16),
            VMEM((3, 512, 256), BF16),
            VMEM((3, 1024, 256), BF16),
            VMEM((3, 1024, 256), BF16),
            VMEM((4, 67, 80, 128), F32),
            VMEM((7 * NB * 8, 128), F32),
            VMEM((7, 7, 7, NB, 128), BF16),
            VMEM((2, 7, 7, NB, 128), BF16),
            VMEM((1, 7, 7, NB, 128), BF16),
            VMEM((12, 6, 6, 2, NB, 128), BF16),
            VMEM((10, 5, 5, 2, NB, 128), BF16),
            VMEM((3, 3, 3, NB, 128), F32),
            VMEM((3, 3, 3, 2, NB, 128), F32),
            VMEM((512, 256), BF16),
            VMEM((256, 256), BF16),
            VMEM((8, 256, 256), BF16),
            VMEM((8, 32, 2, NB, 128), BF16),
            VMEM((8, 32, 2, NB, 128), BF16),
            VMEM((4, 2048, 128), BF16),
            SMEM((2, NB), jnp.int32),
            DMA((4,)),
            DMA((3,)),
            DMA((2,)),
            DMA((2,)),
            DMA((3,)),
            DMA((3,)),
            DMA((8,)),
            DMA((8,)),
            DMA((8, 15)),
            DMA((8, 15)),
        ],
        compiler_params=pltpu.CompilerParams(
            collective_id=0, has_side_effects=True, vmem_limit_bytes=56 << 20
        ),
        name="decode",
    )(ids, owner, latents, wu, w1, w2, near)


def hand_over(rows):
    def body(in_ref, out_ref, held, in_sem, out_sem):
        parts = [(i // 2, pl.ds(i % 2 * 1024, 1024)) for i in range(8)]
        loads = [pltpu.make_async_copy(in_ref.at[p], held.at[p], in_sem.at[i]) for i, p in enumerate(parts)]
        stores = [pltpu.make_async_copy(held.at[p], out_ref.at[p], out_sem.at[i]) for i, p in enumerate(parts)]
        for c in loads:
            c.start()
        for c, d in zip(loads, stores):
            c.wait()
            d.start()
        for d in stores:
            d.wait()

    hbm = pl.BlockSpec(memory_space=pl.ANY)
    return pl.pallas_call(
        body,
        in_specs=[hbm],
        out_specs=hbm,
        out_shape=jax.ShapeDtypeStruct(rows.shape, rows.dtype),
        scratch_shapes=[VMEM(rows.shape, rows.dtype), DMA((8,)), DMA((8,))],
        name="hand_over",
    )(rows)


def local(latents, up_weight, first_weight, second_weight, brick_ids, brick_owner, neighbor_live):
    turned = jnp.swapaxes(up_weight, 3, 4)
    rows = decode(brick_ids, brick_owner, latents, turned, first_weight, second_weight, neighbor_live)
    rows = hand_over(rows)
    return rows.reshape(4, 256, 8, 128).transpose(0, 2, 1, 3).reshape(32, 32768)


def solution(mesh):
    rows = P(("shape", "grp"))
    in_specs = (rows, P(), P(), P(), rows, rows, rows)
    return jax.shard_map(local, mesh=mesh, in_specs=in_specs, out_specs=rows, check_vma=False)
```

```python
import jax
import jax.numpy as jnp
from jax import lax
from jax.experimental import pallas as pl
from jax.experimental.pallas import tpu as pltpu
from jax.sharding import PartitionSpec as P

G = 64
HB = 4
NB = 16
VMEM = pltpu.VMEM
SMEM = pltpu.SMEM
DMA = pltpu.SemaphoreType.DMA
F32 = jnp.float32
BF16 = jnp.bfloat16
MESH = pl.DeviceIdType.MESH

PEERS = sorted(
    ((dy, dx) for dy in range(4) for dx in range(4) if dy or dx),
    key=lambda s: -(min(s[0], 4 - s[0]) + min(s[1], 4 - s[1])),
)
UP_TAP = ((1, 2), (None, 0))
EXT_ORDER = (2, 3, 4, 5, 6, 7, 8, 1, 0, 9, 10, 11)
HID_ORDER = (2, 3, 4, 5, 6, 1, 0, 7, 8, 9)
OUT_ORDER = (2, 3, 4, 1, 0, 5, 6, 7)


def kernel(
    ids,
    owner,
    lat_hbm,
    wu_hbm,
    w1_hbm,
    w2_hbm,
    near_ref,
    out_ref,
    lat,
    wu_raw,
    w1_raw,
    w2_raw,
    wu,
    w1,
    w2,
    pan,
    win,
    reg,
    to_prev,
    to_next,
    ext,
    hid,
    emask,
    hmask,
    pick,
    turn,
    done,
    send,
    recv,
    stage,
    near_ids,
    lat_sem,
    w_sem,
    id_send,
    id_recv,
    halo_send,
    halo_recv,
    own_sem,
    out_sem,
    send_sem,
    recv_sem,
):
    count = lax.axis_size("grp")
    me = lax.axis_index("grp")
    row, col = me // 4, me % 4
    after, before = (me + 1) % count, (me + count - 1) % count
    across = G // HB

    def peer(dy, dx):
        return (row + dy) % 4 * 4 + (col + dx) % 4

    barrier = pltpu.get_barrier_semaphore()
    for dy, dx in PEERS:
        pl.semaphore_signal(barrier, inc=1, device_id={"grp": peer(dy, dx)}, device_id_type=MESH)

    def lat_copy(p):
        return pltpu.make_async_copy(lat_hbm.at[p], lat.at[p], lat_sem.at[p])

    w_copies = [
        pltpu.make_async_copy(s, d, w_sem.at[i])
        for i, (s, d) in enumerate(((wu_hbm, wu_raw), (w1_hbm, w1_raw), (w2_hbm, w2_raw)))
    ]
    for p in (0, 1, 3):
        lat_copy(p).start()
    w_copies[0].start()
    w_copies[1].start()
    lat_copy(2).start()
    w_copies[2].start()

    def border(p, _):
        pan[p, 0] = jnp.zeros(pan.shape[2:], F32)
        pan[p, 65:67] = jnp.zeros((2,) + pan.shape[2:], F32)
        pan[p, :, 0:8] = jnp.zeros((67, 8, 128), F32)
        pan[p, :, 72:80] = jnp.zeros((67, 8, 128), F32)
        return 0

    lax.fori_loop(0, 4, border, 0)

    def load_plane(p):
        lat_copy(p).wait()
        pan[p, 1:65, 8:72] = lat[p].astype(F32)

    def gather(p, id_of, dst, q):
        for b in range(NB):
            local = jnp.maximum(id_of(b), 0)
            by = local // across % across
            bz = local % across
            for j in range(7):
                win[(j * NB + b) * 8 : (j * NB + b) * 8 + 8, :] = pan[p, 4 * by + j, pl.ds(4 * bz + 7, 8), :]
        for j in range(7):
            for l in range(7):
                dst[q, j, l] = win[pl.ds(j * 128 + l, NB, stride=8), :].astype(BF16)

    pl.semaphore_wait(barrier, len(PEERS))
    id_up = pltpu.make_async_remote_copy(
        ids, near_ids.at[0], id_send.at[0], id_recv.at[0], device_id={"grp": after}, device_id_type=MESH
    )
    id_down = pltpu.make_async_remote_copy(
        ids, near_ids.at[1], id_send.at[1], id_recv.at[1], device_id={"grp": before}, device_id_type=MESH
    )
    id_up.start()
    id_down.start()

    halo_up = pltpu.make_async_remote_copy(
        to_next, reg.at[pl.ds(0, 1)], halo_send.at[0], halo_recv.at[0], device_id={"grp": after}, device_id_type=MESH
    )
    halo_down = [
        pltpu.make_async_remote_copy(
            to_prev.at[i],
            reg.at[5 + i],
            halo_send.at[1 + i],
            halo_recv.at[1 + i],
            device_id={"grp": before},
            device_id_type=MESH,
        )
        for i in range(2)
    ]
    load_plane(0)
    gather(0, lambda b: ids[b], reg, 1)
    load_plane(1)
    id_up.wait()
    for p in range(2):
        gather(p, lambda b: near_ids[0, b], to_prev, p)
        halo_down[p].start()
    load_plane(3)
    id_down.wait()
    gather(3, lambda b: near_ids[1, b], to_next, 0)
    halo_up.start()
    gather(1, lambda b: ids[b], reg, 2)
    load_plane(2)
    gather(2, lambda b: ids[b], reg, 3)

    entry = lax.broadcasted_iota(jnp.int32, (NB, 27), 0)
    n = lax.broadcasted_iota(jnp.int32, (NB, 27), 1)
    local = jnp.full((NB, 27), -1, jnp.int32)
    for b in range(NB):
        local = jnp.where(entry == b, ids[b], local)
    used = local >= 0
    local = jnp.maximum(local, 0)
    near_x = me + local // (across * across) + n // 9 - 1
    near_y = local // across % across + n // 3 % 3 - 1
    near_z = local % across + n % 3 - 1
    inside = (near_x >= 0) & (near_x < count) & (near_y >= 0) & (near_y < across)
    inside = inside & (near_z >= 0) & (near_z < across)
    live = jnp.where(inside & ((near_ref[...] > 0) | (n == 13)) & used, 1.0, 0.0)
    for k in range(27):
        emask[k // 9, k // 3 % 3, k % 3] = jnp.broadcast_to(live[:, k : k + 1], (NB, 128))
    w_copies[0].wait()

    def wu_step(kx, _):
        for sy in range(2):
            for sz in range(2):
                parts = []
                for py in range(2):
                    for pz in range(2):
                        ky, kz = UP_TAP[sy][py], UP_TAP[sz][pz]
                        parts.append(
                            jnp.zeros((64, 128), BF16) if ky is None or kz is None else wu_raw[kx, ky, kz]
                        )
                at = (sy * 2 + sz) * 128
                wu[kx, at : at + 128] = jnp.concatenate(parts, 0).T
        return 0

    lax.fori_loop(0, 3, wu_step, 0)

    def patch_weights(src, dst):
        zero = jnp.zeros((64, 64), BF16)

        def tap(kx, ky, kz):
            return src[kx, ky, kz] if 0 <= ky < 3 and 0 <= kz < 3 else zero

        for kx in range(3):
            for ty in range(4):
                for tz in range(4):
                    parts = [tap(kx, ty - py, tz - pz) for py in range(2) for pz in range(2)]
                    at = (ty * 4 + tz) * 64
                    dst[kx, at : at + 64] = jnp.concatenate(parts, 1)

    w_copies[1].wait()
    patch_weights(w1_raw, w1)

    def make_pick():
        col_id = lax.broadcasted_iota(jnp.int32, (512, 256), 1)
        row_id = lax.broadcasted_iota(jnp.int32, (512, 256), 0)
        slot = jnp.full((1, 256), -1, jnp.int32)
        entry = lax.broadcasted_iota(jnp.int32, (1, 256), 1) % NB
        for b in range(NB):
            rank = 0
            for r in range(b):
                rank = rank + jnp.where(owner[r] == owner[b], 1, 0)
            slot = jnp.where(entry == b, jnp.where(ids[b] >= 0, owner[b] * 2 + rank, -1), slot)
        hit = (row_id // NB == slot) & (row_id % NB == col_id // NB)
        pick[...] = jnp.where(hit, 1.0, 0.0).astype(BF16)

    def spread(m, n):
        m = jnp.concatenate([m[0:1]] + [m[1:2]] * (n - 2) + [m[2:3]], 0)
        return jnp.concatenate([m[:, 0:1]] + [m[:, 1:2]] * (n - 2) + [m[:, 2:3]], 1)

    def dot(a, b):
        return jnp.dot(a, b, preferred_element_type=F32)

    def up_plane(e):
        sub = e // 2

        def patch(i):
            return jnp.concatenate(
                [
                    reg[i, sy : sy + 6, sz : sz + 6].reshape(36 * NB, 128)
                    for sy in range(2)
                    for sz in range(2)
                ],
                1,
            )

        if e % 2:
            value = dot(patch(sub), wu[2]) + dot(patch(sub + 1), wu[0])
        else:
            value = dot(patch(sub), wu[1])
        m = spread(emask[(e >= 2) + (e >= 10)], 6)
        for h in range(2):
            part = value[:, h * 128 : h * 128 + 128].reshape(6, 6, NB, 128)
            ext[e, :, :, h] = (part * m).astype(BF16)

    def conv(src, x, n, w_ref):
        total = None
        for kx in range(3):
            patch = jnp.concatenate(
                [
                    src[x + kx, dy : dy + n, dz : dz + n, qy].reshape(n * n * NB, 128)
                    for dy in range(2)
                    for qy in range(2)
                    for dz in range(2)
                ],
                1,
            )
            term = dot(patch, w_ref[kx])
            total = term if total is None else total + term
        return total

    def first_plane(x):
        v = conv(ext, x, 5, w1)
        v = (0.5 * v) * (1.0 + jnp.tanh(0.5 * v))
        m = hmask[(x >= 1) + (x >= 9)]
        for h in range(2):
            part = v[:, h * 128 : h * 128 + 128].reshape(5, 5, NB, 128)
            hid[x, :, :, h] = (part * spread(m[:, :, h], 5)).astype(BF16)

    def second_plane(x):
        v = conv(hid, x, 4, w2)
        own = [ext[x + 2, 1:5, 1:5, h].reshape(16 * NB, 128) for h in range(2)]
        done[x] = (v + jnp.concatenate(own, 1).astype(F32)).astype(BF16)

    def plane_copy(k, x):
        dy, dx = PEERS[k]
        to = peer(dy, dx)
        return pltpu.make_async_remote_copy(
            send.at[x, pl.ds(2 * to, 2)],
            recv.at[x, pl.ds(2 * me, 2)],
            send_sem.at[x, k],
            recv_sem.at[x, k],
            device_id={"grp": to},
            device_id_type=MESH,
        )

    def own_copy(x):
        return pltpu.make_async_copy(send.at[x, pl.ds(2 * me, 2)], recv.at[x, pl.ds(2 * me, 2)], own_sem.at[x])

    def send_plane(x):
        placed = dot(pick[...], done[x]).astype(BF16)
        for h in range(2):
            send[x, :, h] = placed[:, h * 128 : h * 128 + 128].reshape(32, NB, 128)
        for k in range(len(PEERS)):
            plane_copy(k, x).start()
        own_copy(x).start()

    for e in EXT_ORDER[:3]:
        up_plane(e)

    first = lax.broadcasted_iota(jnp.int32, (NB, 128), 1) < 64
    pair = ((0, 1), (1, 1), (1, 2))
    for cx in range(3):
        for cy in range(3):
            for cz in range(3):
                for py in range(2):
                    za, zb = pair[cz]
                    hmask[cx, cy, cz, py] = jnp.where(
                        first, emask[cx, pair[cy][py], za], emask[cx, pair[cy][py], zb]
                    )

    for t in range(10):
        first_plane(HID_ORDER[t])
        if t == 0:
            w_copies[2].wait()
            patch_weights(w2_raw, w2)
        if t == 1:
            make_pick()
        if t >= 2:
            second_plane(OUT_ORDER[t - 2])
            send_plane(OUT_ORDER[t - 2])
        if t + 3 < 12:
            e = EXT_ORDER[t + 3]
            if e == 7:
                gather(3, lambda b: ids[b], reg, 4)
            if e == 1:
                halo_up.wait_recv()
            if e == 9:
                for c in halo_down:
                    c.wait_recv()

                @pl.when(me == count - 1)
                def _():
                    reg[5:7] = jnp.zeros((2,) + reg.shape[1:], BF16)

            up_plane(e)

    i = lax.broadcasted_iota(jnp.int32, (256, 256), 0)
    j = lax.broadcasted_iota(jnp.int32, (256, 256), 1)
    hit = (i // 8 % NB == j % NB) & (i // 128 * 8 + i % 8 == j // NB)
    turn[...] = jnp.where(hit, 1.0, 0.0).astype(BF16)

    def out_copy(x):
        cells = pl.ds(x * 256, 256)
        return pltpu.make_async_copy(stage.at[:, cells], out_ref.at[:, cells], out_sem.at[x])

    def arrive(n, _):
        x = jnp.where(n < 3, n + 2, jnp.where(n < 5, 4 - n, n))
        own_copy(x).wait()
        for k in range(len(PEERS)):
            plane_copy(k, x).wait()
        for half in range(2):
            rows = [recv[x, half * 16 : half * 16 + 16, h].reshape(256, 128) for h in range(2)]
            v = dot(turn[...], jnp.concatenate(rows, 1)).astype(BF16)
            for block in range(2):
                for cy in range(4):
                    for h in range(2):
                        at = block * 128 + cy * 32
                        to = pl.multiple_of(x * 256 + (2 * cy + h) * 32, 32)
                        stage[2 * half + block, pl.ds(to, 32)] = v[at : at + 32, h * 128 : h * 128 + 128]
        out_copy(x).start()
        return 0

    lax.fori_loop(0, 8, arrive, 0)
    halo_up.wait_send()
    for c in halo_down:
        c.wait_send()
    for x in range(8):
        out_copy(x).wait()


def decode(ids, owner, latents, wu, w1, w2, near):
    smem = pl.BlockSpec(memory_space=SMEM)
    hbm = pl.BlockSpec(memory_space=pl.ANY)
    return pl.pallas_call(
        kernel,
        in_specs=[smem, smem, hbm, hbm, hbm, hbm, pl.BlockSpec(memory_space=VMEM)],
        out_specs=hbm,
        out_shape=jax.ShapeDtypeStruct((4, 2048, 128), BF16),
        scratch_shapes=[
            VMEM((4, G, G, 128), BF16),
            VMEM((3, 3, 3, 64, 128), BF16),
            VMEM((3, 3, 3, 64, 64), BF16),
            VMEM((3, 3, 3, 64, 64), BF16),
            VMEM((3, 512, 256), BF16),
            VMEM((3, 1024, 256), BF16),
            VMEM((3, 1024, 256), BF16),
            VMEM((4, 67, 80, 128), F32),
            VMEM((7 * NB * 8, 128), F32),
            VMEM((7, 7, 7, NB, 128), BF16),
            VMEM((2, 7, 7, NB, 128), BF16),
            VMEM((1, 7, 7, NB, 128), BF16),
            VMEM((12, 6, 6, 2, NB, 128), BF16),
            VMEM((10, 5, 5, 2, NB, 128), BF16),
            VMEM((3, 3, 3, NB, 128), F32),
            VMEM((3, 3, 3, 2, NB, 128), F32),
            VMEM((512, 256), BF16),
            VMEM((256, 256), BF16),
            VMEM((8, 256, 256), BF16),
            VMEM((8, 32, 2, NB, 128), BF16),
            VMEM((8, 32, 2, NB, 128), BF16),
            VMEM((4, 2048, 128), BF16),
            SMEM((2, NB), jnp.int32),
            DMA((4,)),
            DMA((3,)),
            DMA((2,)),
            DMA((2,)),
            DMA((3,)),
            DMA((3,)),
            DMA((8,)),
            DMA((8,)),
            DMA((8, 15)),
            DMA((8, 15)),
        ],
        compiler_params=pltpu.CompilerParams(
            collective_id=0, has_side_effects=True, vmem_limit_bytes=56 << 20
        ),
        name="decode",
    )(ids, owner, latents, wu, w1, w2, near)


def hand_over(rows):
    def body(in_ref, out_ref, held, in_sem, out_sem):
        parts = [(i // 2, pl.ds(i % 2 * 1024, 1024)) for i in range(8)]
        loads = [pltpu.make_async_copy(in_ref.at[p], held.at[p], in_sem.at[i]) for i, p in enumerate(parts)]
        stores = [pltpu.make_async_copy(held.at[p], out_ref.at[p], out_sem.at[i]) for i, p in enumerate(parts)]
        for c in loads:
            c.start()
        for c, d in zip(loads, stores):
            c.wait()
            d.start()
        for d in stores:
            d.wait()

    hbm = pl.BlockSpec(memory_space=pl.ANY)
    return pl.pallas_call(
        body,
        in_specs=[hbm],
        out_specs=hbm,
        out_shape=jax.ShapeDtypeStruct(rows.shape, rows.dtype),
        scratch_shapes=[VMEM(rows.shape, rows.dtype), DMA((8,)), DMA((8,))],
        name="hand_over",
    )(rows)


def local(latents, up_weight, first_weight, second_weight, brick_ids, brick_owner, neighbor_live):
    turned = jnp.swapaxes(up_weight, 3, 4)
    rows = decode(brick_ids, brick_owner, latents, turned, first_weight, second_weight, neighbor_live)
    rows = hand_over(rows)
    return rows.reshape(4, 256, 8, 128).transpose(0, 2, 1, 3).reshape(32, 32768)


def solution(mesh):
    rows = P(("shape", "grp"))
    in_specs = (rows, P(), P(), P(), rows, rows, rows)
    return jax.shard_map(local, mesh=mesh, in_specs=in_specs, out_specs=rows, check_vma=False)
```

```python
import jax
import jax.numpy as jnp
from jax import lax
from jax.experimental import pallas as pl
from jax.experimental.pallas import tpu as pltpu
from jax.sharding import PartitionSpec as P

G = 64
HB = 4
NB = 16
VMEM = pltpu.VMEM
SMEM = pltpu.SMEM
DMA = pltpu.SemaphoreType.DMA
F32 = jnp.float32
BF16 = jnp.bfloat16
MESH = pl.DeviceIdType.MESH

PEERS = sorted(
    ((dy, dx) for dy in range(4) for dx in range(4) if dy or dx),
    key=lambda s: -(min(s[0], 4 - s[0]) + min(s[1], 4 - s[1])),
)
UP_TAP = ((1, 2), (None, 0))
EXT_ORDER = (2, 3, 4, 5, 6, 7, 8, 1, 0, 9, 10, 11)
HID_ORDER = (2, 3, 4, 5, 6, 1, 0, 7, 8, 9)
OUT_ORDER = (2, 3, 4, 1, 0, 5, 6, 7)


def kernel(
    ids,
    owner,
    lat_hbm,
    wu_hbm,
    w1_hbm,
    w2_hbm,
    near_ref,
    out_ref,
    lat,
    wu_raw,
    w1_raw,
    w2_raw,
    wu,
    w1,
    w2,
    pan,
    win,
    reg,
    to_prev,
    to_next,
    ext,
    hid,
    emask,
    hmask,
    pick,
    turn,
    done,
    send,
    recv,
    near_ids,
    lat_sem,
    w_sem,
    id_send,
    id_recv,
    halo_send,
    halo_recv,
    own_sem,
    send_sem,
    recv_sem,
):
    count = lax.axis_size("grp")
    me = lax.axis_index("grp")
    row, col = me // 4, me % 4
    after, before = (me + 1) % count, (me + count - 1) % count
    across = G // HB

    def peer(dy, dx):
        return (row + dy) % 4 * 4 + (col + dx) % 4

    barrier = pltpu.get_barrier_semaphore()
    for dy, dx in PEERS:
        pl.semaphore_signal(barrier, inc=1, device_id={"grp": peer(dy, dx)}, device_id_type=MESH)

    def lat_copy(p):
        return pltpu.make_async_copy(lat_hbm.at[p], lat.at[p], lat_sem.at[p])

    w_copies = [
        pltpu.make_async_copy(s, d, w_sem.at[i])
        for i, (s, d) in enumerate(((wu_hbm, wu_raw), (w1_hbm, w1_raw), (w2_hbm, w2_raw)))
    ]
    for p in (0, 1, 3):
        lat_copy(p).start()
    w_copies[0].start()
    w_copies[1].start()
    lat_copy(2).start()
    w_copies[2].start()

    def border(p, _):
        pan[p, 0] = jnp.zeros(pan.shape[2:], F32)
        pan[p, 65:67] = jnp.zeros((2,) + pan.shape[2:], F32)
        pan[p, :, 0:8] = jnp.zeros((67, 8, 128), F32)
        pan[p, :, 72:80] = jnp.zeros((67, 8, 128), F32)
        return 0

    lax.fori_loop(0, 4, border, 0)

    def load_plane(p):
        lat_copy(p).wait()
        pan[p, 1:65, 8:72] = lat[p].astype(F32)

    def gather(p, id_of, dst, q):
        for b in range(NB):
            local = jnp.maximum(id_of(b), 0)
            by = local // across % across
            bz = local % across
            for j in range(7):
                win[(j * NB + b) * 8 : (j * NB + b) * 8 + 8, :] = pan[p, 4 * by + j, pl.ds(4 * bz + 7, 8), :]
        for j in range(7):
            for l in range(7):
                dst[q, j, l] = win[pl.ds(j * 128 + l, NB, stride=8), :].astype(BF16)

    pl.semaphore_wait(barrier, len(PEERS))
    id_up = pltpu.make_async_remote_copy(
        ids, near_ids.at[0], id_send.at[0], id_recv.at[0], device_id={"grp": after}, device_id_type=MESH
    )
    id_down = pltpu.make_async_remote_copy(
        ids, near_ids.at[1], id_send.at[1], id_recv.at[1], device_id={"grp": before}, device_id_type=MESH
    )
    id_up.start()
    id_down.start()

    halo_up = pltpu.make_async_remote_copy(
        to_next, reg.at[pl.ds(0, 1)], halo_send.at[0], halo_recv.at[0], device_id={"grp": after}, device_id_type=MESH
    )
    halo_down = [
        pltpu.make_async_remote_copy(
            to_prev.at[i],
            reg.at[5 + i],
            halo_send.at[1 + i],
            halo_recv.at[1 + i],
            device_id={"grp": before},
            device_id_type=MESH,
        )
        for i in range(2)
    ]
    load_plane(0)
    gather(0, lambda b: ids[b], reg, 1)
    load_plane(1)
    id_up.wait()
    for p in range(2):
        gather(p, lambda b: near_ids[0, b], to_prev, p)
        halo_down[p].start()
    load_plane(3)
    id_down.wait()
    gather(3, lambda b: near_ids[1, b], to_next, 0)
    halo_up.start()
    gather(1, lambda b: ids[b], reg, 2)
    load_plane(2)
    gather(2, lambda b: ids[b], reg, 3)

    entry = lax.broadcasted_iota(jnp.int32, (NB, 27), 0)
    n = lax.broadcasted_iota(jnp.int32, (NB, 27), 1)
    local = jnp.full((NB, 27), -1, jnp.int32)
    for b in range(NB):
        local = jnp.where(entry == b, ids[b], local)
    used = local >= 0
    local = jnp.maximum(local, 0)
    near_x = me + local // (across * across) + n // 9 - 1
    near_y = local // across % across + n // 3 % 3 - 1
    near_z = local % across + n % 3 - 1
    inside = (near_x >= 0) & (near_x < count) & (near_y >= 0) & (near_y < across)
    inside = inside & (near_z >= 0) & (near_z < across)
    live = jnp.where(inside & ((near_ref[...] > 0) | (n == 13)) & used, 1.0, 0.0)
    for k in range(27):
        emask[k // 9, k // 3 % 3, k % 3] = jnp.broadcast_to(live[:, k : k + 1], (NB, 128))
    w_copies[0].wait()

    def wu_step(kx, _):
        for sy in range(2):
            for sz in range(2):
                parts = []
                for py in range(2):
                    for pz in range(2):
                        ky, kz = UP_TAP[sy][py], UP_TAP[sz][pz]
                        parts.append(
                            jnp.zeros((64, 128), BF16) if ky is None or kz is None else wu_raw[kx, ky, kz]
                        )
                at = (sy * 2 + sz) * 128
                wu[kx, at : at + 128] = jnp.concatenate(parts, 0).T
        return 0

    lax.fori_loop(0, 3, wu_step, 0)

    def patch_weights(src, dst):
        zero = jnp.zeros((64, 64), BF16)

        def tap(kx, ky, kz):
            return src[kx, ky, kz] if 0 <= ky < 3 and 0 <= kz < 3 else zero

        for kx in range(3):
            for ty in range(4):
                for tz in range(4):
                    parts = [tap(kx, ty - py, tz - pz) for py in range(2) for pz in range(2)]
                    at = (ty * 4 + tz) * 64
                    dst[kx, at : at + 64] = jnp.concatenate(parts, 1)

    w_copies[1].wait()
    patch_weights(w1_raw, w1)

    def make_pick():
        col_id = lax.broadcasted_iota(jnp.int32, (512, 256), 1)
        row_id = lax.broadcasted_iota(jnp.int32, (512, 256), 0)
        slot = jnp.full((1, 256), -1, jnp.int32)
        entry = lax.broadcasted_iota(jnp.int32, (1, 256), 1) % NB
        for b in range(NB):
            rank = 0
            for r in range(b):
                rank = rank + jnp.where(owner[r] == owner[b], 1, 0)
            slot = jnp.where(entry == b, jnp.where(ids[b] >= 0, owner[b] * 2 + rank, -1), slot)
        hit = (row_id // NB == slot) & (row_id % NB == col_id // NB)
        pick[...] = jnp.where(hit, 1.0, 0.0).astype(BF16)

    def spread(m, n):
        m = jnp.concatenate([m[0:1]] + [m[1:2]] * (n - 2) + [m[2:3]], 0)
        return jnp.concatenate([m[:, 0:1]] + [m[:, 1:2]] * (n - 2) + [m[:, 2:3]], 1)

    def dot(a, b):
        return jnp.dot(a, b, preferred_element_type=F32)

    def up_plane(e):
        sub = e // 2

        def patch(i):
            return jnp.concatenate(
                [
                    reg[i, sy : sy + 6, sz : sz + 6].reshape(36 * NB, 128)
                    for sy in range(2)
                    for sz in range(2)
                ],
                1,
            )

        if e % 2:
            value = dot(patch(sub), wu[2]) + dot(patch(sub + 1), wu[0])
        else:
            value = dot(patch(sub), wu[1])
        m = spread(emask[(e >= 2) + (e >= 10)], 6)
        for h in range(2):
            part = value[:, h * 128 : h * 128 + 128].reshape(6, 6, NB, 128)
            ext[e, :, :, h] = (part * m).astype(BF16)

    def conv(src, x, n, w_ref):
        total = None
        for kx in range(3):
            patch = jnp.concatenate(
                [
                    src[x + kx, dy : dy + n, dz : dz + n, qy].reshape(n * n * NB, 128)
                    for dy in range(2)
                    for qy in range(2)
                    for dz in range(2)
                ],
                1,
            )
            term = dot(patch, w_ref[kx])
            total = term if total is None else total + term
        return total

    def first_plane(x):
        v = conv(ext, x, 5, w1)
        v = (0.5 * v) * (1.0 + jnp.tanh(0.5 * v))
        m = hmask[(x >= 1) + (x >= 9)]
        for h in range(2):
            part = v[:, h * 128 : h * 128 + 128].reshape(5, 5, NB, 128)
            hid[x, :, :, h] = (part * spread(m[:, :, h], 5)).astype(BF16)

    def second_plane(x):
        v = conv(hid, x, 4, w2)
        own = [ext[x + 2, 1:5, 1:5, h].reshape(16 * NB, 128) for h in range(2)]
        done[x] = (v + jnp.concatenate(own, 1).astype(F32)).astype(BF16)

    def plane_copy(k, x):
        dy, dx = PEERS[k]
        to = peer(dy, dx)
        return pltpu.make_async_remote_copy(
            send.at[x, pl.ds(2 * to, 2)],
            recv.at[x, pl.ds(2 * me, 2)],
            send_sem.at[x, k],
            recv_sem.at[x, k],
            device_id={"grp": to},
            device_id_type=MESH,
        )

    def own_copy(x):
        return pltpu.make_async_copy(send.at[x, pl.ds(2 * me, 2)], recv.at[x, pl.ds(2 * me, 2)], own_sem.at[x])

    def send_plane(x):
        placed = dot(pick[...], done[x]).astype(BF16)
        for h in range(2):
            send[x, :, h] = placed[:, h * 128 : h * 128 + 128].reshape(32, NB, 128)
        for k in range(len(PEERS)):
            plane_copy(k, x).start()
        own_copy(x).start()

    for e in EXT_ORDER[:3]:
        up_plane(e)

    first = lax.broadcasted_iota(jnp.int32, (NB, 128), 1) < 64
    pair = ((0, 1), (1, 1), (1, 2))
    for cx in range(3):
        for cy in range(3):
            for cz in range(3):
                for py in range(2):
                    za, zb = pair[cz]
                    hmask[cx, cy, cz, py] = jnp.where(
                        first, emask[cx, pair[cy][py], za], emask[cx, pair[cy][py], zb]
                    )

    for t in range(10):
        first_plane(HID_ORDER[t])
        if t == 0:
            w_copies[2].wait()
            patch_weights(w2_raw, w2)
        if t == 1:
            make_pick()
        if t >= 2:
            second_plane(OUT_ORDER[t - 2])
            send_plane(OUT_ORDER[t - 2])
        if t + 3 < 12:
            e = EXT_ORDER[t + 3]
            if e == 7:
                gather(3, lambda b: ids[b], reg, 4)
            if e == 1:
                halo_up.wait_recv()
            if e == 9:
                for c in halo_down:
                    c.wait_recv()

                @pl.when(me == count - 1)
                def _():
                    reg[5:7] = jnp.zeros((2,) + reg.shape[1:], BF16)

            up_plane(e)

    i = lax.broadcasted_iota(jnp.int32, (256, 256), 0)
    j = lax.broadcasted_iota(jnp.int32, (256, 256), 1)
    hit = (i // 8 % NB == j % NB) & (i // 128 * 8 + i % 8 == j // NB)
    turn[...] = jnp.where(hit, 1.0, 0.0).astype(BF16)

    def arrive(n, _):
        x = jnp.where(n < 3, n + 2, jnp.where(n < 5, 4 - n, n))
        own_copy(x).wait()
        for k in range(len(PEERS)):
            plane_copy(k, x).wait()
        for half in range(2):
            rows = [recv[x, half * 16 : half * 16 + 16, h].reshape(256, 128) for h in range(2)]
            v = dot(turn[...], jnp.concatenate(rows, 1)).astype(BF16)
            for block in range(2):
                for cy in range(4):
                    for h in range(2):
                        at = block * 128 + cy * 32
                        to = pl.multiple_of(x * 256 + (2 * cy + h) * 32, 32)
                        out_ref[2 * half + block, pl.ds(to, 32)] = v[at : at + 32, h * 128 : h * 128 + 128]
        return 0

    lax.fori_loop(0, 8, arrive, 0)
    halo_up.wait_send()
    for c in halo_down:
        c.wait_send()


def decode(ids, owner, latents, wu, w1, w2, near):
    smem = pl.BlockSpec(memory_space=SMEM)
    hbm = pl.BlockSpec(memory_space=pl.ANY)
    return pl.pallas_call(
        kernel,
        in_specs=[smem, smem, hbm, hbm, hbm, hbm, pl.BlockSpec(memory_space=VMEM)],
        out_specs=pl.BlockSpec(memory_space=VMEM),
        out_shape=VMEM((4, 2048, 128), BF16),
        scratch_shapes=[
            VMEM((4, G, G, 128), BF16),
            VMEM((3, 3, 3, 64, 128), BF16),
            VMEM((3, 3, 3, 64, 64), BF16),
            VMEM((3, 3, 3, 64, 64), BF16),
            VMEM((3, 512, 256), BF16),
            VMEM((3, 1024, 256), BF16),
            VMEM((3, 1024, 256), BF16),
            VMEM((4, 67, 80, 128), F32),
            VMEM((7 * NB * 8, 128), F32),
            VMEM((7, 7, 7, NB, 128), BF16),
            VMEM((2, 7, 7, NB, 128), BF16),
            VMEM((1, 7, 7, NB, 128), BF16),
            VMEM((12, 6, 6, 2, NB, 128), BF16),
            VMEM((10, 5, 5, 2, NB, 128), BF16),
            VMEM((3, 3, 3, NB, 128), F32),
            VMEM((3, 3, 3, 2, NB, 128), F32),
            VMEM((512, 256), BF16),
            VMEM((256, 256), BF16),
            VMEM((8, 256, 256), BF16),
            VMEM((8, 32, 2, NB, 128), BF16),
            VMEM((8, 32, 2, NB, 128), BF16),
            SMEM((2, NB), jnp.int32),
            DMA((4,)),
            DMA((3,)),
            DMA((2,)),
            DMA((2,)),
            DMA((3,)),
            DMA((3,)),
            DMA((8,)),
            DMA((8, 15)),
            DMA((8, 15)),
        ],
        compiler_params=pltpu.CompilerParams(
            collective_id=0, has_side_effects=True, vmem_limit_bytes=56 << 20
        ),
        name="decode",
    )(ids, owner, latents, wu, w1, w2, near)


def local(latents, up_weight, first_weight, second_weight, brick_ids, brick_owner, neighbor_live):
    turned = jnp.swapaxes(up_weight, 3, 4)
    rows = decode(brick_ids, brick_owner, latents, turned, first_weight, second_weight, neighbor_live)
    return rows.reshape(4, 256, 8, 128).transpose(0, 2, 1, 3).reshape(32, 32768)


def solution(mesh):
    rows = P(("shape", "grp"))
    in_specs = (rows, P(), P(), P(), rows, rows, rows)
    return jax.shard_map(local, mesh=mesh, in_specs=in_specs, out_specs=rows, check_vma=False)
```

```python
import jax
import jax.numpy as jnp
from jax import lax
from jax.experimental import pallas as pl
from jax.experimental.pallas import tpu as pltpu
from jax.sharding import PartitionSpec as P

G = 64
HB = 4
NB = 16
VMEM = pltpu.VMEM
SMEM = pltpu.SMEM
DMA = pltpu.SemaphoreType.DMA
F32 = jnp.float32
BF16 = jnp.bfloat16
MESH = pl.DeviceIdType.MESH

PEERS = sorted(
    ((dy, dx) for dy in range(4) for dx in range(4) if dy or dx),
    key=lambda s: (-min(s[1], 4 - s[1]), -min(s[0], 4 - s[0])),
)
UP_TAP = ((1, 2), (None, 0))
EXT_ORDER = (2, 3, 4, 5, 6, 7, 8, 1, 0, 9, 10, 11)
HID_ORDER = (2, 3, 4, 5, 6, 1, 0, 7, 8, 9)
OUT_ORDER = (2, 3, 4, 1, 0, 5, 6, 7)


def kernel(
    ids,
    owner,
    lat_hbm,
    wu_hbm,
    w1_hbm,
    w2_hbm,
    near_ref,
    out_ref,
    lat,
    wu_raw,
    w1_raw,
    w2_raw,
    wu,
    w1,
    w2,
    pan,
    win,
    reg,
    to_prev,
    to_next,
    ext,
    hid,
    emask,
    hmask,
    pick,
    turn,
    done,
    send,
    recv,
    near_ids,
    lat_sem,
    w_sem,
    id_send,
    id_recv,
    halo_send,
    halo_recv,
    own_sem,
    send_sem,
    recv_sem,
):
    count = lax.axis_size("grp")
    me = lax.axis_index("grp")
    row, col = me // 4, me % 4
    after, before = (me + 1) % count, (me + count - 1) % count
    across = G // HB

    def peer(dy, dx):
        return (row + dy) % 4 * 4 + (col + dx) % 4

    barrier = pltpu.get_barrier_semaphore()
    for dy, dx in PEERS:
        pl.semaphore_signal(barrier, inc=1, device_id={"grp": peer(dy, dx)}, device_id_type=MESH)

    def lat_copy(p):
        return pltpu.make_async_copy(lat_hbm.at[p], lat.at[p], lat_sem.at[p])

    w_copies = [
        pltpu.make_async_copy(s, d, w_sem.at[i])
        for i, (s, d) in enumerate(((wu_hbm, wu_raw), (w1_hbm, w1_raw), (w2_hbm, w2_raw)))
    ]
    for p in (0, 1, 3):
        lat_copy(p).start()
    w_copies[0].start()
    w_copies[1].start()
    lat_copy(2).start()
    w_copies[2].start()

    def load_plane(p):
        lat_copy(p).wait()
        pan[p, 1:65, 8:72] = lat[p].astype(F32)

    def gather(p, id_of, dst, q):
        for b in range(NB):
            local = jnp.maximum(id_of(b), 0)
            by = local // across % across
            bz = local % across
            for j in range(7):
                win[(j * NB + b) * 8 : (j * NB + b) * 8 + 8, :] = pan[p, 4 * by + j, pl.ds(4 * bz + 7, 8), :]
        for j in range(7):
            for l in range(7):
                dst[q, j, l] = win[pl.ds(j * 128 + l, NB, stride=8), :].astype(BF16)

    pl.semaphore_wait(barrier, len(PEERS))
    id_up = pltpu.make_async_remote_copy(
        ids, near_ids.at[0], id_send.at[0], id_recv.at[0], device_id={"grp": after}, device_id_type=MESH
    )
    id_down = pltpu.make_async_remote_copy(
        ids, near_ids.at[1], id_send.at[1], id_recv.at[1], device_id={"grp": before}, device_id_type=MESH
    )
    id_up.start()
    id_down.start()

    halo_up = pltpu.make_async_remote_copy(
        to_next, reg.at[pl.ds(0, 1)], halo_send.at[0], halo_recv.at[0], device_id={"grp": after}, device_id_type=MESH
    )
    halo_down = [
        pltpu.make_async_remote_copy(
            to_prev.at[i],
            reg.at[5 + i],
            halo_send.at[1 + i],
            halo_recv.at[1 + i],
            device_id={"grp": before},
            device_id_type=MESH,
        )
        for i in range(2)
    ]
    def border(p, _):
        pan[p, 0] = jnp.zeros(pan.shape[2:], F32)
        pan[p, 65:67] = jnp.zeros((2,) + pan.shape[2:], F32)
        pan[p, :, 0:8] = jnp.zeros((67, 8, 128), F32)
        pan[p, :, 72:80] = jnp.zeros((67, 8, 128), F32)
        return 0

    lax.fori_loop(0, 4, border, 0)

    load_plane(0)
    gather(0, lambda b: ids[b], reg, 1)
    load_plane(1)
    id_up.wait()
    for p in range(2):
        gather(p, lambda b: near_ids[0, b], to_prev, p)
        halo_down[p].start()
    load_plane(3)
    id_down.wait()
    gather(3, lambda b: near_ids[1, b], to_next, 0)
    halo_up.start()
    gather(1, lambda b: ids[b], reg, 2)
    load_plane(2)
    gather(2, lambda b: ids[b], reg, 3)

    entry = lax.broadcasted_iota(jnp.int32, (NB, 27), 0)
    n = lax.broadcasted_iota(jnp.int32, (NB, 27), 1)
    local = jnp.full((NB, 27), -1, jnp.int32)
    for b in range(NB):
        local = jnp.where(entry == b, ids[b], local)
    used = local >= 0
    local = jnp.maximum(local, 0)
    near_x = me + local // (across * across) + n // 9 - 1
    near_y = local // across % across + n // 3 % 3 - 1
    near_z = local % across + n % 3 - 1
    inside = (near_x >= 0) & (near_x < count) & (near_y >= 0) & (near_y < across)
    inside = inside & (near_z >= 0) & (near_z < across)
    live = jnp.where(inside & ((near_ref[...] > 0) | (n == 13)) & used, 1.0, 0.0)
    for k in range(27):
        emask[k // 9, k // 3 % 3, k % 3] = jnp.broadcast_to(live[:, k : k + 1], (NB, 128))
    w_copies[0].wait()

    def wu_step(kx, _):
        for sy in range(2):
            for sz in range(2):
                parts = []
                for py in range(2):
                    for pz in range(2):
                        ky, kz = UP_TAP[sy][py], UP_TAP[sz][pz]
                        parts.append(
                            jnp.zeros((64, 128), BF16) if ky is None or kz is None else wu_raw[kx, ky, kz]
                        )
                at = (sy * 2 + sz) * 128
                wu[kx, at : at + 128] = jnp.concatenate(parts, 0).T
        return 0

    lax.fori_loop(0, 3, wu_step, 0)

    def patch_weights(src, dst):
        zero = jnp.zeros((64, 64), BF16)

        def tap(kx, ky, kz):
            return src[kx, ky, kz] if 0 <= ky < 3 and 0 <= kz < 3 else zero

        for kx in range(3):
            for ty in range(4):
                for tz in range(4):
                    parts = [tap(kx, ty - py, tz - pz) for py in range(2) for pz in range(2)]
                    at = (ty * 4 + tz) * 64
                    dst[kx, at : at + 64] = jnp.concatenate(parts, 1)

    w_copies[1].wait()
    patch_weights(w1_raw, w1)

    def make_pick():
        col_id = lax.broadcasted_iota(jnp.int32, (512, 256), 1)
        row_id = lax.broadcasted_iota(jnp.int32, (512, 256), 0)
        slot = jnp.full((1, 256), -1, jnp.int32)
        entry = lax.broadcasted_iota(jnp.int32, (1, 256), 1) % NB
        for b in range(NB):
            rank = 0
            for r in range(b):
                rank = rank + jnp.where(owner[r] == owner[b], 1, 0)
            slot = jnp.where(entry == b, jnp.where(ids[b] >= 0, owner[b] * 2 + rank, -1), slot)
        hit = (row_id // NB == slot) & (row_id % NB == col_id // NB)
        pick[...] = jnp.where(hit, 1.0, 0.0).astype(BF16)

    def spread(m, n):
        m = jnp.concatenate([m[0:1]] + [m[1:2]] * (n - 2) + [m[2:3]], 0)
        return jnp.concatenate([m[:, 0:1]] + [m[:, 1:2]] * (n - 2) + [m[:, 2:3]], 1)

    def dot(a, b):
        return jnp.dot(a, b, preferred_element_type=F32)

    def up_plane(e):
        sub = e // 2

        def patch(i):
            return jnp.concatenate(
                [
                    reg[i, sy : sy + 6, sz : sz + 6].reshape(36 * NB, 128)
                    for sy in range(2)
                    for sz in range(2)
                ],
                1,
            )

        if e % 2:
            value = dot(patch(sub), wu[2]) + dot(patch(sub + 1), wu[0])
        else:
            value = dot(patch(sub), wu[1])
        m = spread(emask[(e >= 2) + (e >= 10)], 6)
        for h in range(2):
            part = value[:, h * 128 : h * 128 + 128].reshape(6, 6, NB, 128)
            ext[e, :, :, h] = (part * m).astype(BF16)

    def conv(src, x, n, w_ref):
        total = None
        for kx in range(3):
            patch = jnp.concatenate(
                [
                    src[x + kx, dy : dy + n, dz : dz + n, qy].reshape(n * n * NB, 128)
                    for dy in range(2)
                    for qy in range(2)
                    for dz in range(2)
                ],
                1,
            )
            term = dot(patch, w_ref[kx])
            total = term if total is None else total + term
        return total

    def first_plane(x):
        v = conv(ext, x, 5, w1)
        v = (0.5 * v) * (1.0 + jnp.tanh(0.5 * v))
        m = hmask[(x >= 1) + (x >= 9)]
        for h in range(2):
            part = v[:, h * 128 : h * 128 + 128].reshape(5, 5, NB, 128)
            hid[x, :, :, h] = (part * spread(m[:, :, h], 5)).astype(BF16)

    def second_plane(x):
        v = conv(hid, x, 4, w2)
        own = [ext[x + 2, 1:5, 1:5, h].reshape(16 * NB, 128) for h in range(2)]
        done[x] = (v + jnp.concatenate(own, 1).astype(F32)).astype(BF16)

    def plane_copy(k, x):
        dy, dx = PEERS[k]
        to = peer(dy, dx)
        return pltpu.make_async_remote_copy(
            send.at[x, pl.ds(2 * to, 2)],
            recv.at[x, pl.ds(2 * me, 2)],
            send_sem.at[x, k],
            recv_sem.at[x, k],
            device_id={"grp": to},
            device_id_type=MESH,
        )

    def own_copy(x):
        return pltpu.make_async_copy(send.at[x, pl.ds(2 * me, 2)], recv.at[x, pl.ds(2 * me, 2)], own_sem.at[x])

    def send_plane(x):
        placed = dot(pick[...], done[x]).astype(BF16)
        for h in range(2):
            send[x, :, h] = placed[:, h * 128 : h * 128 + 128].reshape(32, NB, 128)
        for k in range(len(PEERS)):
            plane_copy(k, x).start()
        own_copy(x).start()

    for e in EXT_ORDER[:3]:
        up_plane(e)

    first = lax.broadcasted_iota(jnp.int32, (NB, 128), 1) < 64
    pair = ((0, 1), (1, 1), (1, 2))
    for cx in range(3):
        for cy in range(3):
            for cz in range(3):
                for py in range(2):
                    za, zb = pair[cz]
                    hmask[cx, cy, cz, py] = jnp.where(
                        first, emask[cx, pair[cy][py], za], emask[cx, pair[cy][py], zb]
                    )

    for t in range(10):
        first_plane(HID_ORDER[t])
        if t == 0:
            w_copies[2].wait()
            patch_weights(w2_raw, w2)
        if t == 1:
            make_pick()
        if t >= 2:
            second_plane(OUT_ORDER[t - 2])
            send_plane(OUT_ORDER[t - 2])
        if t + 3 < 12:
            e = EXT_ORDER[t + 3]
            if e == 7:
                gather(3, lambda b: ids[b], reg, 4)
            if e == 1:
                halo_up.wait_recv()
            if e == 9:
                for c in halo_down:
                    c.wait_recv()

                @pl.when(me == count - 1)
                def _():
                    reg[5:7] = jnp.zeros((2,) + reg.shape[1:], BF16)

            up_plane(e)

    i = lax.broadcasted_iota(jnp.int32, (256, 256), 0)
    j = lax.broadcasted_iota(jnp.int32, (256, 256), 1)
    hit = (i // 8 % NB == j % NB) & (i // 128 * 8 + i % 8 == j // NB)
    turn[...] = jnp.where(hit, 1.0, 0.0).astype(BF16)

    def arrive(n, _):
        x = jnp.where(n < 3, n + 2, jnp.where(n < 5, 4 - n, n))
        own_copy(x).wait()
        for k in range(len(PEERS)):
            plane_copy(k, x).wait()
        for half in range(2):
            rows = [recv[x, half * 16 : half * 16 + 16, h].reshape(256, 128) for h in range(2)]
            v = dot(turn[...], jnp.concatenate(rows, 1)).astype(BF16)
            for block in range(2):
                for cy in range(4):
                    for h in range(2):
                        at = block * 128 + cy * 32
                        to = pl.multiple_of(x * 256 + (2 * cy + h) * 32, 32)
                        out_ref[2 * half + block, pl.ds(to, 32)] = v[at : at + 32, h * 128 : h * 128 + 128]
        return 0

    lax.fori_loop(0, 8, arrive, 0)
    halo_up.wait_send()
    for c in halo_down:
        c.wait_send()


def decode(ids, owner, latents, wu, w1, w2, near):
    smem = pl.BlockSpec(memory_space=SMEM)
    hbm = pl.BlockSpec(memory_space=pl.ANY)
    return pl.pallas_call(
        kernel,
        in_specs=[smem, smem, hbm, hbm, hbm, hbm, pl.BlockSpec(memory_space=VMEM)],
        out_specs=pl.BlockSpec(memory_space=VMEM),
        out_shape=VMEM((4, 2048, 128), BF16),
        scratch_shapes=[
            VMEM((4, G, G, 128), BF16),
            VMEM((3, 3, 3, 64, 128), BF16),
            VMEM((3, 3, 3, 64, 64), BF16),
            VMEM((3, 3, 3, 64, 64), BF16),
            VMEM((3, 512, 256), BF16),
            VMEM((3, 1024, 256), BF16),
            VMEM((3, 1024, 256), BF16),
            VMEM((4, 67, 80, 128), F32),
            VMEM((7 * NB * 8, 128), F32),
            VMEM((7, 7, 7, NB, 128), BF16),
            VMEM((2, 7, 7, NB, 128), BF16),
            VMEM((1, 7, 7, NB, 128), BF16),
            VMEM((12, 6, 6, 2, NB, 128), BF16),
            VMEM((10, 5, 5, 2, NB, 128), BF16),
            VMEM((3, 3, 3, NB, 128), F32),
            VMEM((3, 3, 3, 2, NB, 128), F32),
            VMEM((512, 256), BF16),
            VMEM((256, 256), BF16),
            VMEM((8, 256, 256), BF16),
            VMEM((8, 32, 2, NB, 128), BF16),
            VMEM((8, 32, 2, NB, 128), BF16),
            SMEM((2, NB), jnp.int32),
            DMA((4,)),
            DMA((3,)),
            DMA((2,)),
            DMA((2,)),
            DMA((3,)),
            DMA((3,)),
            DMA((8,)),
            DMA((8, 15)),
            DMA((8, 15)),
        ],
        compiler_params=pltpu.CompilerParams(
            collective_id=0, has_side_effects=True, vmem_limit_bytes=56 << 20
        ),
        name="decode",
    )(ids, owner, latents, wu, w1, w2, near)


def local(latents, up_weight, first_weight, second_weight, brick_ids, brick_owner, neighbor_live):
    turned = jnp.swapaxes(up_weight, 3, 4)
    rows = decode(brick_ids, brick_owner, latents, turned, first_weight, second_weight, neighbor_live)
    return rows.reshape(4, 256, 8, 128).transpose(0, 2, 1, 3).reshape(32, 32768)


def solution(mesh):
    rows = P(("shape", "grp"))
    in_specs = (rows, P(), P(), P(), rows, rows, rows)
    return jax.shard_map(local, mesh=mesh, in_specs=in_specs, out_specs=rows, check_vma=False)
```
